128 devices in a mesh: dp: 32 (over y, x, core), rep: 4 (over z).
Axes of the slice: x: 4, y: 4, z: 4, core: 2. Of those that a mesh axis runs over, the one named last changes fastest.
Arguments:
- tokens: bfloat16 [512, 512, 1024], P(('dp', 'rep')), may hold values from -6 to 6
- token_counts: int32 [512], P(('dp', 'rep')), may hold values from 1 to 512
- segment_ids: int32 [512, 512], P(('dp', 'rep')), may hold values from 0 to 7, never falling along the last dimension, each value on 1 to 128 neighbouring positions
- dest_device: int32 [2048], P(('dp', 'rep')), may hold values from 0 to 31, as said below
- dest_slot: int32 [2048], P(('dp', 'rep')), may hold values from 0 to 15, as said below
- cotangent: bfloat16 [262144, 2048], P(('dp', 'rep')), may hold values from -384 to 384
- master_weight: float32 [1024, 2048], P('dp'), as said below
- momentum: float32 [1024, 2048], replicated, may hold values from -6 to 6
- variance: float32 [1024, 2048], P('dp'), may hold values from 0.25 to 4
Outputs:
- new_weights: bfloat16 [1024, 2048], replicated
- new_momentum: float32 [1024, 2048], P('dp')
- lamb_step: float32 [1024, 2048], P('dp')
The draws below stay inside these ranges and needn't reach their ends.
Inputs may be any that keep to these rules, and one draw needn't show every extreme that they name: `dest_device`: for each replica group, every block goes to a dp index; one device sends at most 1 block to any one device of its replica group, so its 16 blocks go to 16 different dp indices; every device receives exactly 16 blocks. `dest_slot`: the blocks received by one device have distinct slots, so all 16 slots are filled. `master_weight`: master weights, fan-in scaled, finite.
All inputs are finite; a program needn't handle non-finite values. Where the reference program divides by a largest or mean magnitude, that divisor is 1e-20 or more.
Results may differ from the reference program's by a relative error of at most 0.0075.
Values may be sent and summed in bfloat16 or wider, within the bound.
A program may use at most 128 MiB of HBM per device.

```python
import math
import jax
import jax.numpy as jnp
import numpy as np
from jax import lax

D = 1024
FFW = 2048
SEQ = 512
BLOCK = 128
TOK_DEV = 2048
BLOCKS_DEV = 16
ROWS = 512
N_DP = 32
N_REP = 4


def route_tables(key):

    def one_group(group_key):
        first, second, third, fourth = jax.random.split(group_key, 4)
        order_one = jax.random.permutation(first, N_DP)
        order_two = jax.random.permutation(second, N_DP)
        offsets = jax.random.permutation(third, N_DP)
        block_ids = jnp.arange(BLOCKS_DEV)
        shifted = offsets[block_ids % N_DP]
        receiver = order_two[(order_one[:, None] + shifted[None, :]) % N_DP]
        slot_orders = jax.vmap(lambda item_key: jax.random.permutation(item_key, BLOCKS_DEV))(jax.random.split(fourth, N_DP))
        slots = slot_orders[receiver, jnp.broadcast_to(block_ids[None, :], receiver.shape)]
        return (receiver, slots)
    receivers, slot_table = jax.vmap(one_group)(jax.random.split(key, N_REP))
    receivers = jnp.transpose(receivers, (1, 0, 2)).reshape(-1).astype(jnp.int32)
    slot_table = jnp.transpose(slot_table, (1, 0, 2)).reshape(-1).astype(jnp.int32)
    return (receivers, slot_table)


def draw_dest_device(key, part):
    receivers, slot_table = route_tables(key)
    return receivers


def draw_dest_slot(key, part):
    receivers, slot_table = route_tables(key)
    return slot_table


def draw_master_weight(key, part):
    key = jax.random.fold_in(key, 11)
    base_key, column_key = jax.random.split(key)
    row_factor = 10.0 ** (jnp.arange(D, dtype=jnp.float32) / D)
    column_factor = jnp.exp(jax.random.uniform(column_key, (FFW,), jnp.float32, 0.0, math.log(10.0)))
    base = jnp.clip(jax.random.normal(base_key, (D, FFW), jnp.float32), -5.0, 5.0)
    return base * row_factor[:, None] * column_factor[None, :] * (0.2 / math.sqrt(D))


def with_ends(drawn, key, least, top_value):
    longest = drawn.shape.index(max(drawn.shape))
    spots = []
    for shift in (0, 1):
        where = [jax.random.randint(jax.random.fold_in(key, axis), (), 0, length) for axis, length in enumerate(drawn.shape)]
        where[longest] = (where[longest] + shift) % drawn.shape[longest]
        spots.append(tuple(where))
    return drawn.at[spots[0]].set(least).at[spots[1]].set(top_value)


def block_levels(stream_key, extent, pieces, smallest, top_value):
    def one(dim, parts):
        steps = jax.random.uniform(jax.random.fold_in(jax.random.fold_in(stream_key, 6), dim), (parts,), jnp.float32, smallest / len(pieces), top_value / len(pieces))
        return jnp.repeat(jnp.exp(steps), extent[dim] // parts).reshape((-1,) + (1,) * (len(extent) - dim - 1))

    factor_of = one(*pieces[0])
    for cut in pieces[1:]:
        factor_of = factor_of * one(*cut)
    return factor_of


def length_profile(count, total, reach, skew):
    loads = [(1 << 20) // math.isqrt(rank ** skew) + 1 for rank in range(2, count + 1)]
    rest, counts = total - reach - (count - 1), [1] * (count - 1)
    while rest > 0:
        movable = [i for i in range(count - 1) if counts[i] < reach]
        whole, left = sum([loads[i] for i in movable]), rest
        for i in movable:
            more = min(reach - counts[i], max(1, left * loads[i] // whole), rest)
            counts[i] = counts[i] + more
            rest = rest - more
    return np.array([reach] + counts)


def uneven(own_key, number_of, total, limit, slope):
    if number_of == 2:
        one = jax.random.randint(own_key, (), max(1, total - limit), min(limit, total - 1) + 1)
        return jnp.stack([one, total - one])
    sizes = jnp.asarray(length_profile(number_of, total, limit, slope), jnp.int32)
    pairs = (number_of - 1) // 2
    giver, sink = sizes[1:1 + 2 * pairs:2], sizes[2:2 + 2 * pairs:2]
    margin = jnp.minimum(giver - 1, limit - sink)
    moved = jax.random.randint(jax.random.fold_in(own_key, 1), (pairs,), 0, 1 << 20) % (margin + 1)
    sizes = sizes.at[1:1 + 2 * pairs:2].set(giver - moved).at[2:2 + 2 * pairs:2].set(sink + moved)
    return sizes[jax.random.permutation(jax.random.fold_in(own_key, 2), number_of)]


def gaussian(key, dims, width, bound, pieces=(), kind=jnp.bfloat16):
    result = width * jax.random.normal(key, dims, jnp.float32)
    if pieces:
        result = result * block_levels(key, dims, pieces, -0.22, 0.18)
    return jnp.clip(result, -bound, bound).astype(kind)


def setup_inputs(seed: int = 0) -> dict:
    key_list = jax.random.split(jax.random.key(seed), 10)
    tokens = gaussian(key_list[0], (ROWS, SEQ, D), 1.0, 6.0, ((0, 128),))
    token_counts = with_ends(jax.random.randint(key_list[1], (ROWS,), 1, SEQ + 1), jax.random.fold_in(key_list[1], 1), 1, SEQ).astype(jnp.int32)
    segment_ids = jax.vmap(lambda own: jnp.searchsorted(jnp.cumsum(uneven(own, 8, SEQ, SEQ // 4, 0)), jnp.arange(SEQ), side="right"))(jax.random.split(key_list[2], ROWS)).reshape((ROWS, SEQ)).astype(jnp.int32)
    dest_device = draw_dest_device(jax.random.fold_in(key_list[9], 71), 0)
    dest_slot = draw_dest_slot(jax.random.fold_in(key_list[9], 71), 0)
    cotangent = gaussian(key_list[5], (TOK_DEV * N_DP * N_REP, FFW), 64.0, 384.0, ((0, 128),))
    master_weight = draw_master_weight(jax.random.fold_in(key_list[9], 71), 0)
    momentum = gaussian(key_list[7], (D, FFW), 1.0, 6.0, (), jnp.float32)
    variance = jnp.clip(jnp.exp(math.log(4.0) - 2.7725887 * jax.random.uniform(key_list[8], (D, FFW), jnp.float32) ** block_levels(key_list[8], (D, FFW), ((0, 32),), -0.2, 0.2)), 0.25, 4.0)
    return {"tokens": tokens, "token_counts": token_counts, "segment_ids": segment_ids, "dest_device": dest_device, "dest_slot": dest_slot, "cotangent": cotangent, "master_weight": master_weight, "momentum": momentum, "variance": variance}


root_half = 0.7071067811865476
normal_peak = 0.3989422804014327
momentum_decay = 0.9
learn_rate = 0.05
epsilon = 1e-06

def segment_lengths(segment_ids, token_counts):
    position = lax.broadcasted_iota(jnp.int32, segment_ids.shape, 1)
    living = position < token_counts[:, None]
    matched = (segment_ids[:, :, None] == segment_ids[:, None, :]) & living[:, None, :]
    return jnp.where(living, lax.optimization_barrier(jnp.sum(matched, axis=2, dtype=jnp.int32)), 0)

def gelu_slope(preact):
    return 0.5 * (1.0 + lax.erf(preact * root_half)) + preact * jnp.exp(-0.5 * preact * preact) * normal_peak

def server_step(average, owned_variance):
    row_scale = lax.optimization_barrier(jnp.mean(jnp.abs(average), axis=1))
    moment = row_scale[:, None] * jnp.tanh(average / (row_scale + epsilon)[:, None])
    return (moment, moment / (jnp.sqrt(owned_variance) + epsilon))

def reference(tokens, token_counts, segment_ids, dest_device, dest_slot, cotangent, master_weight, momentum, variance):
    lengths = segment_lengths(segment_ids, token_counts)
    token_weight = jnp.where(lengths > 0, 1.0 / jnp.maximum(lengths, 1).astype(jnp.float32), 0.0).astype(jnp.float32)
    blocks = tokens.reshape(N_DP, N_REP, BLOCKS_DEV, BLOCK, D)
    block_weight = token_weight.reshape(N_DP, N_REP, BLOCKS_DEV, BLOCK)
    target = dest_device.reshape(N_DP, N_REP, BLOCKS_DEV).astype(jnp.int32)
    slot_index = dest_slot.reshape(N_DP, N_REP, BLOCKS_DEV).astype(jnp.int32)
    replica = jnp.broadcast_to(jnp.arange(N_REP, dtype=jnp.int32)[None, :, None], target.shape)
    placed = jnp.zeros((N_DP, N_REP, BLOCKS_DEV, BLOCK, D), jnp.bfloat16).at[target, replica, slot_index].set(blocks)
    placed_weight = jnp.zeros((N_DP, N_REP, BLOCKS_DEV, BLOCK), jnp.float32).at[target, replica, slot_index].set(block_weight)
    local_tokens = placed.reshape(N_DP * N_REP, TOK_DEV, D)
    local_weight = placed_weight.reshape(N_DP * N_REP, TOK_DEV)
    local_cot = cotangent.reshape(N_DP * N_REP, TOK_DEV, FFW)
    weights = lax.optimization_barrier(master_weight.astype(jnp.bfloat16)).astype(jnp.float32)

    def device_term(total, item):
        inputs, weight_row, cot_rows = item
        inputs_wide = inputs.astype(jnp.float32)
        preact = jnp.dot(inputs_wide, weights, precision=lax.Precision.HIGHEST)
        delta = (cot_rows.astype(jnp.float32) * gelu_slope(preact) * weight_row[:, None]).astype(jnp.bfloat16)
        grad = jnp.dot(inputs_wide.T, delta.astype(jnp.float32), precision=lax.Precision.HIGHEST)
        moment = momentum_decay * momentum + (1.0 - momentum_decay) * grad
        row_scale = lax.optimization_barrier(jnp.mean(jnp.abs(moment), axis=1))
        unit = lax.optimization_barrier(jnp.tanh(moment / (row_scale + epsilon)[:, None]).astype(jnp.bfloat16))
        sent_scale = lax.optimization_barrier(row_scale.astype(jnp.bfloat16))
        return (total + sent_scale.astype(jnp.float32)[:, None] * unit.astype(jnp.float32), None)
    summed, unused = lax.scan(device_term, jnp.zeros((D, FFW), jnp.float32), (local_tokens, local_weight, local_cot))
    average = summed / (N_DP * N_REP)
    new_momentum, direction = server_step(average, variance)
    ratio = jnp.sqrt(jnp.sum(master_weight * master_weight)) / (jnp.sqrt(jnp.sum(direction * direction)) + epsilon)
    lamb_step = ratio * direction
    new_weights = (master_weight - learn_rate * lamb_step).astype(jnp.bfloat16)
    return (new_weights, new_momentum, lamb_step)
```

```python
import functools

import jax
import jax.numpy as jnp
from jax import lax
from jax.experimental import pallas as pl
from jax.experimental.pallas import tpu as pltpu
from jax.sharding import PartitionSpec as P

MESH = pl.DeviceIdType.MESH
F32 = jnp.float32
BF16 = jnp.bfloat16
momentum_decay = 0.9
learn_rate = 0.05
epsilon = 1e-06
normal_peak = 0.3989422804014327

GROUPS = (
    ((0, 1), (0, 3), (1, 0), (3, 0)),
    ((1, 1), (3, 3)),
    ((1, 3), (3, 1)),
    ((0, 2), (2, 0)),
    ((1, 2), (3, 2), (2, 1), (2, 3)),
    ((2, 2),),
)
MOVES = [(0, 0, 0), (0, 0, 1)]
for group in GROUPS:
    for core in (0, 1):
        for dy, dx in group:
            MOVES.append((dy, dx, core))

PER = 4
TILE = 256


def gelu_slope(a):
    u = jnp.abs(a)
    t = 1.0 / (1.0 + u * (0.3275911 * 0.7071067811865476))
    e = jnp.exp(-0.5 * (a * a))
    poly = t * (
        0.5 * 0.254829592
        + t
        * (
            0.5 * -0.284496736
            + t * (0.5 * 1.421413741 + t * (0.5 * -1.453152027 + t * (0.5 * 1.061405429)))
        )
    )
    h = e * (poly - normal_peak * u)
    return jnp.where(a >= 0.0, 1.0 - h, h)


def kernel(
    inv,
    tok_hbm,
    meta,
    cot_hbm,
    master,
    mom_hbm,
    variance,
    out_w,
    out_m,
    out_l,
    tok,
    stage,
    arr,
    cot,
    w,
    acc,
    xt,
    wt,
    metar,
    metas,
    u,
    r1,
    s1,
    r2,
    s2,
    r3,
    r4,
    dirs,
    q,
    lsem,
    tss,
    tsr,
    mss,
    msr,
    gbs,
    gbr,
    gas,
    gar,
    gcs,
    gcr,
    c1s,
    c1r,
    c2s,
    c2r,
    c3s,
    c3r,
    c4s,
    c4r,
    qs,
    qr,
):
    me = lax.axis_index("dp")
    rep = lax.axis_index("rep")
    y = me // 8
    x = (me // 2) % 4
    c = me % 2
    a = (1 - c) * y + c * x
    b = (1 - c) * x + c * y
    sa = 4 * (1 - c) + c
    sb = 4 * c + (1 - c)

    def place(ai, bi):
        return ai * sa + bi * sb

    def copy(src, dst, ss, rs, dev):
        return pltpu.make_async_remote_copy(
            src_ref=src, dst_ref=dst, send_sem=ss, recv_sem=rs, device_id=dev, device_id_type=MESH
        )

    def peer(move):
        dy, dx, dc = move
        return (((y + dy) % 4) * 4 + (x + dx) % 4) * 2 + (c + dc) % 2

    ctok = pltpu.make_async_copy(tok_hbm, tok, lsem.at[0])
    ccot = pltpu.make_async_copy(cot_hbm, cot, lsem.at[1])
    cmom = pltpu.make_async_copy(mom_hbm, acc, lsem.at[2])
    ctok.start()

    barrier = pltpu.get_barrier_semaphore()

    @pl.loop(1, 32)
    def _(k):
        pl.semaphore_signal(barrier, inc=1, device_id=((me + k) % 32, rep), device_id_type=MESH)

    for k in range(1, 4):
        pl.semaphore_signal(barrier, inc=1, device_id=(me, (rep + k) % 4), device_id_type=MESH)
    w[y * 4 + x, c] = master[...].astype(BF16)
    pl.semaphore_wait(barrier, 34)

    def gather_b(g):
        out = []
        for k in range(1, 4):
            mine = w.at[y * 4 + x, c]
            cp = copy(
                mine, mine, gbs.at[g, k - 1], gbr.at[g, k - 1],
                (place(a, (b + k) % 4) * 2 + c, rep),
            )
            cp.start()
            out.append(cp)
        return out

    def gather_a(g):
        out = []
        for k in range(1, 4):
            for bb in range(4):
                part = w.at[place(a, bb), c]
                cp = copy(
                    part, part, gas.at[g, k - 1, bb], gar.at[g, k - 1, bb],
                    (place((a + k) % 4, b) * 2 + c, rep),
                )
                cp.start()
                out.append(cp)
        return out

    def gather_c(g):
        part = w.at[:, c]
        cp = copy(part, part, gcs.at[g], gcr.at[g], (y * 8 + x * 2 + 1 - c, rep))
        cp.start()
        return [cp]

    first = gather_b(0)

    metacopies = []
    for j in range(1, 32):
        p = peer(MOVES[j])
        cp = copy(meta.at[p], metar.at[j], mss.at[j], msr.at[j], (p, rep))
        cp.start()
        metacopies.append(cp)
    metar[0] = meta[me]

    ctok.wait()
    ccot.start()
    cmom.start()
    sends = []

    def send(j):
        p = peer(MOVES[j])
        stage[j] = tok[inv[p]]
        cp = copy(stage.at[j], arr.at[j], tss.at[j], tsr.at[j], (p, rep))
        cp.start()
        sends.append(cp)

    arr[0] = tok[inv[me]]
    for j in range(1, 4):
        send(j)
    for cp in first:
        cp.wait()
    second = gather_a(0)
    for j in range(4, 32):
        send(j)
    for cp in metacopies:
        cp.wait()
    cmeta = pltpu.make_async_copy(metar, metas, lsem.at[3])
    cmeta.start()
    for cp in second:
        cp.wait()
    third = gather_c(0)
    cmom.wait()

    @pl.loop(0, 32)
    def _(i):
        rows = pl.ds(pl.multiple_of(i * 32, 32), 32)
        acc[rows, :] = acc[rows, :] * (momentum_decay / (1.0 - momentum_decay))

    cmeta.wait()
    ccot.wait()
    for cp in third:
        cp.wait()

    def work(ch):
        for i in range(PER):
            j = ch * PER + i
            lens = metar[j][0:1, :]
            weight = jnp.where(lens > 0, 1.0 / jnp.maximum(lens, 1).astype(F32), 0.0)
            wt[i * 128 : (i + 1) * 128, :] = jnp.transpose(jnp.broadcast_to(weight, (128, 128)))
            xt[:, i * 128 : (i + 1) * 128] = jnp.transpose(arr[j])

        @pl.loop(0, 2048 // TILE)
        def _(n):
            cols = pl.ds(pl.multiple_of(n * TILE, TILE), TILE)
            xin = arr[pl.ds(ch * PER, PER)].reshape(PER * 128, 1024)
            pre = jnp.dot(xin, w[:, :, :, cols].reshape(1024, TILE), preferred_element_type=F32)
            parts = []
            for i in range(PER):
                slot = metas[ch * PER + i, 1, 0]
                ci = cot[slot, :, cols].astype(F32)
                rows = slice(i * 128, (i + 1) * 128)
                wcol = wt[rows, :]
                wide = jnp.concatenate([wcol] * (TILE // 128), axis=1)
                parts.append((ci * gelu_slope(pre[rows]) * wide).astype(BF16))
            delta = jnp.concatenate(parts, axis=0)
            acc[:, cols] += jnp.dot(xt[...], delta, preferred_element_type=F32)

    for i in range(1, PER):
        sends[i - 1].wait_recv()
    work(0)

    @pl.loop(1, 32 // PER)
    def _(ch):
        for i in range(PER):
            j = ch * PER + i
            copy(stage.at[j], arr.at[j], tss.at[j], tsr.at[j], (me, (rep + 1) % 4)).wait_recv()
        work(ch)

    for cp in sends:
        cp.wait_send()

    def squeezed(yx, core):
        rows = pl.ds(pl.multiple_of((yx * 2 + core) * 32, 32), 32)
        moment = acc[rows, :] * (1.0 - momentum_decay)
        scale = jnp.sum(jnp.abs(moment), axis=1, keepdims=True) * (1.0 / 2048)
        unit = jnp.tanh(moment / (scale + epsilon))
        return scale.astype(BF16).astype(F32) * unit.astype(BF16).astype(F32)

    other = (y * 8 + x * 2 + 1 - c, rep)

    @pl.loop(0, 16)
    def _(i):
        yx = place((a + 1 + i // 4) % 4, i % 4)
        u[i] = squeezed(yx, 1 - c).astype(BF16)
        copy(u.at[i], r1.at[yx], c1s.at[i], c1r.at[yx], other).start()

    def add_core(k):
        for bb in range(4):
            yx = place((a + k) % 4, bb)
            copy(u.at[0], r1.at[yx], c1s.at[0], c1r.at[yx], other).wait_recv()
            s1[k, bb] = (squeezed(yx, c) + r1[yx].astype(F32)).astype(BF16)

    stage2 = []
    for k in (2, 1, 3, 0):
        add_core(k)
        if k:
            cp = copy(
                s1.at[k], r2.at[k - 1], c2s.at[k - 1], c2r.at[k - 1],
                (place((a + k) % 4, b) * 2 + c, rep),
            )
            cp.start()
            stage2.append(cp)
    for cp in stage2:
        cp.wait()

    def add_a(bi):
        total = s1[0, bi].astype(F32)
        for k in range(3):
            total = total + r2[k, bi].astype(F32)
        return total

    stage3 = []
    for k in (2, 1, 3):
        bi = (b + k) % 4
        s2[k - 1] = add_a(bi).astype(BF16)
        cp = copy(
            s2.at[k - 1], r3.at[k - 1], c3s.at[k - 1], c3r.at[k - 1],
            (place(a, bi) * 2 + c, rep),
        )
        cp.start()
        stage3.append(cp)
    total = add_a(b)
    for cp in stage3:
        cp.wait()
    for k in range(3):
        total = total + r3[k].astype(F32)
    r4[rep] = total.astype(BF16)
    stage4 = []
    for k in (2, 1, 3):
        cp = copy(
            r4.at[rep], r4.at[rep], c4s.at[k - 1], c4r.at[k - 1], (me, (rep + k) % 4)
        )
        cp.start()
        stage4.append(cp)
    for cp in stage4:
        cp.wait()
    average = (
        r4[0].astype(F32) + r4[1].astype(F32) + r4[2].astype(F32) + r4[3].astype(F32)
    ) * (1.0 / 128)
    scale = jnp.sum(jnp.abs(average), axis=1, keepdims=True) * (1.0 / 2048)
    moment = scale * jnp.tanh(average / (scale + epsilon))
    out_m[...] = moment
    direction = moment / (jnp.sqrt(variance[...]) + epsilon)
    dirs[...] = direction

    def folded(v):
        line = jnp.sum(v, axis=0, keepdims=True)
        out = line[:, 0:128]
        for i in range(1, 16):
            out = out + line[:, i * 128 : (i + 1) * 128]
        return out

    q[me] = jnp.concatenate(
        [
            folded(master[...] * master[...]),
            folded(direction * direction),
            jnp.zeros((6, 128), F32),
        ],
        axis=0,
    )
    scalars = []
    for j in range(1, 32):
        cp = copy(q.at[me], q.at[me], qs.at[j], qr.at[j], (peer(MOVES[j]), rep))
        cp.start()
        scalars.append(cp)
    for cp in scalars:
        cp.wait()
    sums = jnp.sum(jnp.sum(q[...], axis=0), axis=1, keepdims=True)
    roots = jnp.sqrt(sums)
    ratio = roots[0:1, :] / (roots[1:2, :] + epsilon)
    step = ratio * dirs[...]
    out_l[...] = step
    w[y * 4 + x, c] = (master[...] - learn_rate * step).astype(BF16)
    for stagefn in (gather_b, gather_a, gather_c):
        for cp in stagefn(1):
            cp.wait()

    @pl.loop(0, 16)
    def _(i):
        copy(u.at[i], r1.at[i], c1s.at[i], c1r.at[i], other).wait_send()

    cout = pltpu.make_async_copy(w, out_w, lsem.at[4])
    cout.start()
    cout.wait()


def run(inv, tokens, meta, cotangent, master, momentum, variance):
    sem = pltpu.SemaphoreType.DMA
    vmem = pl.BlockSpec(memory_space=pltpu.VMEM)
    hbm = pl.BlockSpec(memory_space=pl.ANY)
    return pl.pallas_call(
        kernel,
        out_shape=(
            jax.ShapeDtypeStruct((16, 2, 32, 2048), BF16),
            jax.ShapeDtypeStruct((32, 2048), F32),
            jax.ShapeDtypeStruct((32, 2048), F32),
        ),
        in_specs=[
            pl.BlockSpec(memory_space=pltpu.SMEM),
            hbm,
            vmem,
            hbm,
            vmem,
            hbm,
            vmem,
        ],
        out_specs=(hbm, vmem, vmem),
        scratch_shapes=[
            pltpu.VMEM((16, 128, 1024), BF16),
            pltpu.VMEM((32, 128, 1024), BF16),
            pltpu.VMEM((32, 128, 1024), BF16),
            pltpu.VMEM((16, 128, 2048), BF16),
            pltpu.VMEM((16, 2, 32, 2048), BF16),
            pltpu.VMEM((1024, 2048), F32),
            pltpu.VMEM((1024, PER * 128), BF16),
            pltpu.VMEM((PER * 128, 128), F32),
            pltpu.VMEM((32, 8, 128), jnp.int32),
            pltpu.SMEM((32, 8, 128), jnp.int32),
            pltpu.VMEM((16, 32, 2048), BF16),
            pltpu.VMEM((16, 32, 2048), BF16),
            pltpu.VMEM((4, 4, 32, 2048), BF16),
            pltpu.VMEM((3, 4, 32, 2048), BF16),
            pltpu.VMEM((3, 32, 2048), BF16),
            pltpu.VMEM((3, 32, 2048), BF16),
            pltpu.VMEM((4, 32, 2048), BF16),
            pltpu.VMEM((32, 2048), F32),
            pltpu.VMEM((32, 8, 128), F32),
            sem((5,)),
            sem((32,)),
            sem((32,)),
            sem((32,)),
            sem((32,)),
            sem((2, 3)),
            sem((2, 3)),
            sem((2, 3, 4)),
            sem((2, 3, 4)),
            sem((2,)),
            sem((2,)),
            sem((16,)),
            sem((16,)),
            sem((3,)),
            sem((3,)),
            sem((3,)),
            sem((3,)),
            sem((3,)),
            sem((3,)),
            sem((32,)),
            sem((32,)),
        ],
        compiler_params=pltpu.CompilerParams(
            collective_id=1, has_side_effects=True, vmem_limit_bytes=63 * 2**20
        ),
        cost_estimate=pl.CostEstimate(
            flops=34 * 10**9, bytes_accessed=40 * 10**6, transcendentals=20 * 10**6
        ),
    )(inv, tokens, meta, cotangent, master, momentum, variance)


def per_device(
    tokens,
    token_counts,
    segment_ids,
    dest_device,
    dest_slot,
    cotangent,
    master_weight,
    momentum,
    variance,
):
    position = lax.broadcasted_iota(jnp.int32, segment_ids.shape, 1)
    living = position < token_counts[:, None]
    matched = (segment_ids[:, :, None] == segment_ids[:, None, :]) & living[:, None, :]
    lengths = jnp.where(living, jnp.sum(matched, axis=2, dtype=jnp.int32), 0).reshape(16, 128)
    peers = jnp.arange(32, dtype=jnp.int32)
    chosen = dest_device[None, :] == peers[:, None]
    inv = jnp.sum(jnp.where(chosen, jnp.arange(16, dtype=jnp.int32)[None, :], 0), axis=1)
    slots = jnp.sum(jnp.where(chosen, dest_slot[None, :], 0), axis=1)
    lens = jnp.sum(jnp.where(chosen[:, :, None], lengths[None], 0), axis=1)
    row = lax.broadcasted_iota(jnp.int32, (32, 8, 128), 1)
    meta = jnp.where(row == 0, lens[:, None, :], slots[:, None, None])
    new_w, new_m, step = run(
        inv,
        tokens.reshape(16, 128, 1024),
        meta,
        cotangent.reshape(16, 128, 2048),
        master_weight,
        momentum,
        variance,
    )
    return (new_w.reshape(1024, 2048), new_m, step)


def solution(mesh):
    return jax.shard_map(
        per_device,
        mesh=mesh,
        in_specs=(
            P(("dp", "rep"), None, None),
            P(("dp", "rep")),
            P(("dp", "rep"), None),
            P(("dp", "rep")),
            P(("dp", "rep")),
            P(("dp", "rep"), None),
            P("dp", None),
            P(),
            P("dp", None),
        ),
        out_specs=(P(), P("dp", None), P("dp", None)),
        check_vma=False,
    )
```

```python
import functools

import jax
import jax.numpy as jnp
from jax import lax
from jax.experimental import pallas as pl
from jax.experimental.pallas import tpu as pltpu
from jax.sharding import PartitionSpec as P

MESH = pl.DeviceIdType.MESH
F32 = jnp.float32
BF16 = jnp.bfloat16
momentum_decay = 0.9
learn_rate = 0.05
epsilon = 1e-06
normal_peak = 0.3989422804014327

GROUPS = (
    ((1, 1), (3, 3)),
    ((1, 3), (3, 1)),
    ((0, 2), (2, 0)),
    ((1, 2), (1, 0), (3, 2), (3, 0)),
    ((2, 1), (0, 1), (2, 3), (0, 3)),
    ((2, 2),),
)
MOVES = [(0, 0, 0), (0, 0, 1)]
for group in GROUPS:
    for core in (0, 1):
        for dy, dx in group:
            MOVES.append((dy, dx, core))

STEPS = ((20, 4), (24, 4), (28, 4), (30, 2), (32, 2))
EDGES = (0, 20, 24, 28, 30, 32)
WINDOW = 12
TILE = 512


def gelu_slope(a):
    u = jnp.abs(a)
    d = 1.0 + u * (0.3275911 * 0.7071067811865476)
    t = pl.reciprocal(d, approx=True)
    t = t * (2.0 - d * t)
    e = jnp.exp2((a * a) * (-0.5 * 1.4426950408889634))
    poly = t * (
        0.5 * 0.254829592
        + t
        * (
            0.5 * -0.284496736
            + t * (0.5 * 1.421413741 + t * (0.5 * -1.453152027 + t * (0.5 * 1.061405429)))
        )
    )
    h = e * (poly - normal_peak * u)
    return jnp.where(a >= 0.0, 1.0 - h, h)


def kernel(
    inv,
    tok_hbm,
    meta,
    cot_hbm,
    master,
    mom_hbm,
    variance,
    out_w,
    out_d,
    out_m,
    out_l,
    out_r,
    tok,
    stage,
    arr0,
    arr1,
    arr2,
    arr3,
    arr4,
    cot,
    w,
    acc,
    xs,
    xt,
    wt,
    metar,
    metas,
    orders,
    u,
    r1,
    s1,
    r2,
    s2,
    r3,
    r4,
    q,
    lsem,
    tss,
    tsr,
    mss,
    msr,
    gbs,
    gbr,
    gas,
    gar,
    gzs,
    gzr,
    gcs,
    gcr,
    c1s,
    c1r,
    c2s,
    c2r,
    c3s,
    c3r,
    c4s,
    c4r,
    qs,
    qr,
):
    me = lax.axis_index("dp")
    rep = lax.axis_index("rep")
    y = me // 8
    x = (me // 2) % 4
    c = me % 2
    a = (1 - c) * y + c * x
    b = (1 - c) * x + c * y
    sa = 4 * (1 - c) + c
    sb = 4 * c + (1 - c)
    arrs = (arr0, arr1, arr2, arr3, arr4)

    def place(ai, bi):
        return ai * sa + bi * sb

    def at_a(k):
        return (place((a + k) % 4, b) * 2 + c, rep)

    def at_b(k):
        return (place(a, (b + k) % 4) * 2 + c, rep)

    other = (y * 8 + x * 2 + 1 - c, rep)

    def copy(src, dst, ss, rs, dev):
        return pltpu.make_async_remote_copy(
            src_ref=src, dst_ref=dst, send_sem=ss, recv_sem=rs, device_id=dev, device_id_type=MESH
        )

    def peer(move):
        dy, dx, dc = move
        return (((y + dy) % 4) * 4 + (x + dx) % 4) * 2 + (c + dc) % 2

    def landing(j):
        n = max(i for i in range(5) if EDGES[i] <= j)
        return arrs[n].at[j - EDGES[n]]

    ctok = pltpu.make_async_copy(tok_hbm, tok, lsem.at[0])
    ccot = pltpu.make_async_copy(cot_hbm, cot, lsem.at[1])
    cmom = pltpu.make_async_copy(mom_hbm, acc, lsem.at[2])
    ctok.start()

    w[y * 4 + x, c] = master[...].astype(BF16)
    barrier = pltpu.get_barrier_semaphore()

    @pl.loop(1, 32)
    def _(k):
        pl.semaphore_signal(barrier, inc=1, device_id=((me + k) % 32, rep), device_id_type=MESH)

    for k in range(1, 4):
        pl.semaphore_signal(barrier, inc=1, device_id=(me, (rep + k) % 4), device_id_type=MESH)
    pl.semaphore_wait(barrier, 34)

    quarter = pl.ds(pl.multiple_of(rep * 512, 512), 512)
    gb = []
    for k in range(1, 4):
        part = w.at[y * 4 + x, c, :, quarter]
        gb.append(copy(part, part, gbs.at[0, k - 1], gbr.at[0, k - 1], at_b(k)))
        gb[-1].start()

    metacopies = []
    for j in range(1, 32):
        p = peer(MOVES[j])
        cp = copy(meta.at[p], metar.at[j], mss.at[j], msr.at[j], (p, rep))
        cp.start()
        metacopies.append(cp)
    metar[0] = meta[me]

    ctok.wait()
    ccot.start()
    cmom.start()
    sends = [None]
    arr0[0] = tok[inv[me]]
    ga = []
    gz = []
    gc = []
    for j in range(1, 32):
        if j > WINDOW:
            sends[j - WINDOW].wait_send()
        p = peer(MOVES[j])
        spot = stage.at[(j - 1) % WINDOW]
        spot[...] = tok[inv[p]]
        cp = copy(spot, landing(j), tss.at[j], tsr.at[j], (p, rep))
        cp.start()
        sends.append(cp)
        if j == 4:
            for cp in gb:
                cp.wait()
            for k in range(1, 4):
                for bb in range(4):
                    part = w.at[place(a, bb), c, :, quarter]
                    ga.append(copy(part, part, gas.at[0, k - 1, bb], gar.at[0, k - 1, bb], at_a(k)))
                    ga[-1].start()
        if j == 10:
            for cp in ga:
                cp.wait()
            for k in range(1, 4):
                part = w.at[:, c, :, quarter]
                gz.append(copy(part, part, gzs.at[k - 1], gzr.at[k - 1], (me, (rep + k) % 4)))
                gz[-1].start()
    for cp in metacopies:
        cp.wait()
    cmeta = pltpu.make_async_copy(metar, metas, lsem.at[3])
    cmeta.start()
    cmom.wait()

    @pl.loop(0, 32)
    def _(i):
        rows = pl.ds(pl.multiple_of(i * 32, 32), 32)
        acc[rows, :] = acc[rows, :] * (momentum_decay / (1.0 - momentum_decay))

    cmeta.wait()
    count = jnp.int32(0)
    for j in range(32):
        count = count + jnp.minimum(metas[j, 1, 0], 1)
        orders[16 + j] = count

    @pl.loop(0, 16)
    def _(k):
        found = jnp.int32(0)
        for j in range(32):
            found = found + jnp.where(orders[16 + j] <= k, 1, 0)
        orders[k] = found

    ccot.wait()
    for cp in gz:
        cp.wait()
    part = w.at[:, c]
    cp = copy(part, part, gcs.at[0, 0], gcr.at[0, 0], other)
    cp.start()
    cp.wait()
    cw = pltpu.make_async_copy(w, out_w, lsem.at[5])
    cw.start()

    done = 0
    arrived = 1
    for number, (needed, blocks) in enumerate(STEPS):
        while arrived < needed:
            sends[arrived].wait_recv()
            arrived += 1
        rowcount = blocks * 128
        slots = []
        for i in range(blocks):
            o = jnp.minimum(orders[done + i], 31)
            slots.append(jnp.maximum(metas[o, 1, 0] - 1, 0))
            block = arrs[0][jnp.minimum(o, EDGES[1] - 1)]
            for n in range(1, number + 1):
                at = jnp.clip(o - EDGES[n], 0, EDGES[n + 1] - EDGES[n] - 1)
                block = lax.select(o >= EDGES[n], arrs[n][at], block)
            xs[i * 128 : (i + 1) * 128, :] = block
            xt[:, i * 128 : (i + 1) * 128] = jnp.transpose(block)
            lens = metar[o][0:1, :]
            weight = jnp.where(lens > 0, 1.0 / jnp.maximum(lens, 1).astype(F32), 0.0)
            wt[i * 128 : (i + 1) * 128, :] = jnp.transpose(jnp.broadcast_to(weight, (128, 128)))
        done += blocks

        @pl.loop(0, 2048 // TILE)
        def _(n):
            cols = pl.ds(pl.multiple_of(n * TILE, TILE), TILE)
            pre = jnp.dot(
                xs[0:rowcount, :], w[:, :, :, cols].reshape(1024, TILE), preferred_element_type=F32
            )
            parts = []
            for i in range(blocks):
                rows = slice(i * 128, (i + 1) * 128)
                wide = jnp.concatenate([wt[rows, :]] * (TILE // 128), axis=1)
                ci = cot[slots[i], :, cols].astype(F32)
                parts.append((ci * gelu_slope(pre[rows]) * wide).astype(BF16))
            delta = jnp.concatenate(parts, axis=0)
            acc[:, cols] += jnp.dot(xt[:, 0:rowcount], delta, preferred_element_type=F32)

    cw.wait()
    for j in range(32 - WINDOW, 32):
        sends[j].wait_send()

    def squeezed(yx, core):
        rows = pl.ds(pl.multiple_of((yx * 2 + core) * 32, 32), 32)
        moment = acc[rows, :] * (1.0 - momentum_decay)
        scale = jnp.sum(jnp.abs(moment), axis=1, keepdims=True) * (1.0 / 2048)
        unit = jnp.tanh(moment * (1.0 / (scale + epsilon)))
        return scale.astype(BF16).astype(F32) * unit.astype(BF16).astype(F32)

    @pl.loop(0, 16)
    def _(i):
        yx = place((a + 1 + i // 4) % 4, i % 4)
        u[i] = squeezed(yx, 1 - c).astype(BF16)
        copy(u.at[i], r1.at[yx], c1s.at[i], c1r.at[yx], other).start()

    def add_core(k):
        @pl.loop(0, 4)
        def _(bb):
            yx = place((a + k) % 4, bb)
            copy(u.at[0], r1.at[yx], c1s.at[0], c1r.at[yx], other).wait_recv()
            s1[k, bb] = (squeezed(yx, c) + r1[yx].astype(F32)).astype(BF16)

    stage2 = []
    for k in (2, 1, 3, 0):
        add_core(k)
        if k:
            cp = copy(s1.at[k], r2.at[k - 1], c2s.at[k - 1], c2r.at[k - 1], at_a(k))
            cp.start()
            stage2.append(cp)
    for cp in stage2:
        cp.wait()

    def add_a(bi):
        total = s1[0, bi].astype(F32)
        for k in range(3):
            total = total + r2[k, bi].astype(F32)
        return total

    stage3 = []
    for k in (2, 1, 3):
        s2[k - 1] = add_a((b + k) % 4).astype(BF16)
        cp = copy(s2.at[k - 1], r3.at[k - 1], c3s.at[k - 1], c3r.at[k - 1], at_b(k))
        cp.start()
        stage3.append(cp)
    total = add_a(b)
    for cp in stage3:
        cp.wait()
    for k in range(3):
        total = total + r3[k].astype(F32)
    r4[rep] = total.astype(BF16)
    stage4 = []
    for k in (2, 1, 3):
        cp = copy(r4.at[rep], r4.at[rep], c4s.at[k - 1], c4r.at[k - 1], (me, (rep + k) % 4))
        cp.start()
        stage4.append(cp)
    for cp in stage4:
        cp.wait()
    average = (
        r4[0].astype(F32) + r4[1].astype(F32) + r4[2].astype(F32) + r4[3].astype(F32)
    ) * (1.0 / 128)
    scale = jnp.sum(jnp.abs(average), axis=1, keepdims=True) * (1.0 / 2048)
    moment = scale * jnp.tanh(average / (scale + epsilon))
    out_m[...] = moment
    direction = moment / (jnp.sqrt(variance[...]) + epsilon)
    w[y * 4 + x, c] = direction.astype(BF16)

    def group(ai, bi):
        return w.at[place(ai, bi), c]

    dcopies = []

    def to_a(bi):
        for k in (2, 1, 3):
            cp = copy(group(a, bi), group(a, bi), gas.at[1, k - 1, bi], gar.at[1, k - 1, bi], at_a(k))
            cp.start()
            dcopies.append(cp)

    def to_core(ai, bi):
        yx = place(ai, bi)
        copy(w.at[yx, c], w.at[yx, c], gcs.at[1, yx], gcr.at[1, yx], other).start()

    gb = {}
    for k in (2, 1, 3):
        gb[k] = copy(group(a, b), group(a, b), gbs.at[1, k - 1], gbr.at[1, k - 1], at_b(k))
        gb[k].start()
    to_a(b)

    def folded(v):
        line = jnp.sum(v, axis=0, keepdims=True)
        out = line[:, 0:128]
        for i in range(1, 16):
            out = out + line[:, i * 128 : (i + 1) * 128]
        return out

    q[me] = jnp.concatenate(
        [
            folded(master[...] * master[...]),
            folded(direction * direction),
            jnp.zeros((6, 128), F32),
        ],
        axis=0,
    )
    out_l[...] = direction
    scalars = []
    for j in range(1, 32):
        cp = copy(q.at[me], q.at[me], qs.at[j], qr.at[j], (peer(MOVES[j]), rep))
        cp.start()
        scalars.append(cp)

    to_core(a, b)
    for k in (1, 3, 2):
        gb[k].wait()
        to_a((b - k + 4) % 4)
        to_core(a, (b - k + 4) % 4)
    for cp in scalars:
        cp.wait()
    sums = jnp.sum(jnp.sum(q[...], axis=0), axis=1, keepdims=True)
    roots = jnp.sqrt(sums)
    ratio = roots[0:1, :] / (roots[1:2, :] + epsilon)
    out_l[...] = out_l[...] * ratio
    out_r[...] = jnp.broadcast_to(ratio, (8, 128))

    for k in (1, 3, 2):
        ai = (a - k + 4) % 4

        @pl.loop(0, 4)
        def _(i):
            bi = (b + i) % 4
            copy(group(ai, bi), group(ai, bi), gas.at[1, k - 1, bi], gar.at[1, k - 1, bi], at_a(k)).wait_recv()
            to_core(ai, bi)

    half = pltpu.make_async_copy(w.at[:, c], out_d.at[:, c], lsem.at[4])
    half.start()

    @pl.loop(0, 16)
    def _(i):
        theirs = w.at[i, 1 - c]
        copy(theirs, theirs, gcs.at[1, i], gcr.at[1, i], other).wait_recv()

    rest = pltpu.make_async_copy(w.at[:, 1 - c], out_d.at[:, 1 - c], lsem.at[6])
    rest.start()
    for cp in dcopies:
        cp.wait_send()

    @pl.loop(0, 16)
    def _(i):
        copy(w.at[i, c], w.at[i, c], gcs.at[1, i], gcr.at[1, i], other).wait_send()
        copy(u.at[i], r1.at[i], c1s.at[i], c1r.at[i], other).wait_send()

    half.wait()
    rest.wait()


def run(inv, tokens, meta, cotangent, master, momentum, variance):
    sem = pltpu.SemaphoreType.DMA
    vmem = pl.BlockSpec(memory_space=pltpu.VMEM)
    hbm = pl.BlockSpec(memory_space=pl.ANY)
    return pl.pallas_call(
        kernel,
        out_shape=(
            jax.ShapeDtypeStruct((16, 2, 32, 2048), BF16),
            jax.ShapeDtypeStruct((16, 2, 32, 2048), BF16),
            jax.ShapeDtypeStruct((32, 2048), F32),
            jax.ShapeDtypeStruct((32, 2048), F32),
            jax.ShapeDtypeStruct((8, 128), F32),
        ),
        in_specs=[
            pl.BlockSpec(memory_space=pltpu.SMEM),
            hbm,
            vmem,
            hbm,
            vmem,
            hbm,
            vmem,
        ],
        out_specs=(hbm, hbm, vmem, vmem, vmem),
        scratch_shapes=[
            pltpu.VMEM((16, 128, 1024), BF16),
            pltpu.VMEM((WINDOW, 128, 1024), BF16),
            pltpu.VMEM((20, 128, 1024), BF16),
            pltpu.VMEM((4, 128, 1024), BF16),
            pltpu.VMEM((4, 128, 1024), BF16),
            pltpu.VMEM((2, 128, 1024), BF16),
            pltpu.VMEM((2, 128, 1024), BF16),
            pltpu.VMEM((16, 128, 2048), BF16),
            pltpu.VMEM((16, 2, 32, 2048), BF16),
            pltpu.VMEM((1024, 2048), F32),
            pltpu.VMEM((512, 1024), BF16),
            pltpu.VMEM((1024, 512), BF16),
            pltpu.VMEM((512, 128), F32),
            pltpu.VMEM((32, 8, 128), jnp.int32),
            pltpu.SMEM((32, 8, 128), jnp.int32),
            pltpu.SMEM((48,), jnp.int32),
            pltpu.VMEM((16, 32, 2048), BF16),
            pltpu.VMEM((16, 32, 2048), BF16),
            pltpu.VMEM((4, 4, 32, 2048), BF16),
            pltpu.VMEM((3, 4, 32, 2048), BF16),
            pltpu.VMEM((3, 32, 2048), BF16),
            pltpu.VMEM((3, 32, 2048), BF16),
            pltpu.VMEM((4, 32, 2048), BF16),
            pltpu.VMEM((32, 8, 128), F32),
            sem((7,)),
            sem((32,)),
            sem((32,)),
            sem((32,)),
            sem((32,)),
            sem((2, 3)),
            sem((2, 3)),
            sem((2, 3, 4)),
            sem((2, 3, 4)),
            sem((3,)),
            sem((3,)),
            sem((2, 16)),
            sem((2, 16)),
            sem((16,)),
            sem((16,)),
            sem((3,)),
            sem((3,)),
            sem((3,)),
            sem((3,)),
            sem((3,)),
            sem((3,)),
            sem((32,)),
            sem((32,)),
        ],
        compiler_params=pltpu.CompilerParams(
            collective_id=1, has_side_effects=True, vmem_limit_bytes=63 * 2**20
        ),
        cost_estimate=pl.CostEstimate(
            flops=18 * 10**9, bytes_accessed=40 * 10**6, transcendentals=20 * 10**6
        ),
    )(inv, tokens, meta, cotangent, master, momentum, variance)


def per_device(
    tokens,
    token_counts,
    segment_ids,
    dest_device,
    dest_slot,
    cotangent,
    master_weight,
    momentum,
    variance,
):
    position = lax.broadcasted_iota(jnp.int32, segment_ids.shape, 1)
    living = position < token_counts[:, None]
    matched = (segment_ids[:, :, None] == segment_ids[:, None, :]) & living[:, None, :]
    lengths = jnp.where(living, jnp.sum(matched, axis=2, dtype=jnp.int32), 0).reshape(16, 128)
    peers = jnp.arange(32, dtype=jnp.int32)
    chosen = dest_device[None, :] == peers[:, None]
    inv = jnp.sum(jnp.where(chosen, jnp.arange(16, dtype=jnp.int32)[None, :], 0), axis=1)
    slots = jnp.sum(jnp.where(chosen, dest_slot[None, :] + 1, 0), axis=1)
    lens = jnp.sum(jnp.where(chosen[:, :, None], lengths[None], 0), axis=1)
    row = lax.broadcasted_iota(jnp.int32, (32, 8, 128), 1)
    meta = jnp.where(row == 0, lens[:, None, :], slots[:, None, None])
    old_w, direction, new_m, step, ratio = run(
        inv,
        tokens.reshape(16, 128, 1024),
        meta,
        cotangent.reshape(16, 128, 2048),
        master_weight,
        momentum,
        variance,
    )
    new_w = old_w.astype(F32) - (learn_rate * ratio[0, 0]) * direction.astype(F32)
    return (new_w.astype(BF16).reshape(1024, 2048), new_m, step)


def solution(mesh):
    return jax.shard_map(
        per_device,
        mesh=mesh,
        in_specs=(
            P(("dp", "rep"), None, None),
            P(("dp", "rep")),
            P(("dp", "rep"), None),
            P(("dp", "rep")),
            P(("dp", "rep")),
            P(("dp", "rep"), None),
            P("dp", None),
            P(),
            P("dp", None),
        ),
        out_specs=(P(), P("dp", None), P("dp", None)),
        check_vma=False,
    )
```

```python
import functools

import jax
import jax.numpy as jnp
from jax import lax
from jax.experimental import pallas as pl
from jax.experimental.pallas import tpu as pltpu
from jax.sharding import PartitionSpec as P

MESH = pl.DeviceIdType.MESH
F32 = jnp.float32
BF16 = jnp.bfloat16
momentum_decay = 0.9
learn_rate = 0.05
epsilon = 1e-06
normal_peak = 0.3989422804014327

GROUPS = (
    ((1, 1), (3, 3)),
    ((1, 2), (3, 0)),
    ((2, 1), (0, 3)),
    ((1, 3), (3, 1)),
    ((3, 2), (1, 0)),
    ((2, 3), (0, 1)),
    ((0, 2), (2, 0)),
    ((2, 2),),
)
MOVES = [(0, 0, 0), (0, 0, 1)]
for group in GROUPS:
    for core in (0, 1):
        for dy, dx in group:
            MOVES.append((dy, dx, core))

EDGES = (0, 18, 20, 22, 24, 26, 28, 30, 32)
BUFFERS = len(EDGES) - 1
WINDOW = 16
TILE = 1024


def gelu_slope(a):
    u = jnp.abs(a)
    d = 1.0 + u * (0.3275911 * 0.7071067811865476)
    t = pl.reciprocal(d, approx=True)
    t = t * (2.0 - d * t)
    e = jnp.exp2((a * a) * (-0.5 * 1.4426950408889634))
    poly = t * (
        0.5 * 0.254829592
        + t
        * (
            0.5 * -0.284496736
            + t * (0.5 * 1.421413741 + t * (0.5 * -1.453152027 + t * (0.5 * 1.061405429)))
        )
    )
    h = e * (poly - normal_peak * u)
    return jnp.where(a >= 0.0, 1.0 - h, h)


def kernel(
    counts,
    dest,
    dslot,
    segments,
    tok_hbm,
    cot_hbm,
    master,
    mom_hbm,
    variance,
    out_w,
    out_m,
    out_l,
    tok,
    stage,
    arr0,
    arr1,
    arr2,
    arr3,
    arr4,
    arr5,
    arr6,
    arr7,
    cot,
    w,
    gathered,
    acc,
    xs,
    xt,
    wt,
    metar,
    metas,
    orders,
    table,
    lengths,
    metasent,
    u,
    r1,
    s1,
    r2,
    s2,
    r3,
    r4,
    q,
    lsem,
    outsem,
    tss,
    tsr,
    mss,
    msr,
    gbs,
    gbr,
    gas,
    gar,
    gzs,
    gzr,
    gcs,
    gcr,
    c1s,
    c1r,
    c2s,
    c2r,
    c3s,
    c3r,
    c4s,
    c4r,
    qs,
    qr,
):
    me = lax.axis_index("dp")
    rep = lax.axis_index("rep")
    y = me // 8
    x = (me // 2) % 4
    c = me % 2
    a = (1 - c) * y + c * x
    b = (1 - c) * x + c * y
    sa = 4 * (1 - c) + c
    sb = 4 * c + (1 - c)
    arrs = (arr0, arr1, arr2, arr3, arr4, arr5, arr6, arr7)

    def place(ai, bi):
        return ai * sa + bi * sb

    def at_a(k):
        return (place((a + k) % 4, b) * 2 + c, rep)

    def at_b(k):
        return (place(a, (b + k) % 4) * 2 + c, rep)

    other = (y * 8 + x * 2 + 1 - c, rep)

    def copy(src, dst, ss, rs, dev):
        return pltpu.make_async_remote_copy(
            src_ref=src, dst_ref=dst, send_sem=ss, recv_sem=rs, device_id=dev, device_id_type=MESH
        )

    def peer(move):
        dy, dx, dc = move
        return (((y + dy) % 4) * 4 + (x + dx) % 4) * 2 + (c + dc) % 2

    def landing(j):
        n = max(i for i in range(BUFFERS) if EDGES[i] <= j)
        return arrs[n].at[j - EDGES[n]]

    ctok = pltpu.make_async_copy(tok_hbm, tok, lsem.at[0])
    ccot = pltpu.make_async_copy(cot_hbm, cot, lsem.at[1])
    cmom = pltpu.make_async_copy(mom_hbm, acc, lsem.at[2])
    ctok.start()

    w[y * 4 + x, c] = master[...].astype(BF16)
    barrier = pltpu.get_barrier_semaphore()

    @pl.loop(1, 32)
    def _(k):
        pl.semaphore_signal(barrier, inc=1, device_id=((me + k) % 32, rep), device_id_type=MESH)

    for k in range(1, 4):
        pl.semaphore_signal(barrier, inc=1, device_id=(me, (rep + k) % 4), device_id_type=MESH)

    @pl.loop(0, 32)
    def _(p):
        block, there, slot = jnp.int32(0), jnp.int32(0), jnp.int32(0)
        for i in range(16):
            same = jnp.where(dest[i] == p, 1, 0)
            block = block + same * i
            there = there + same
            slot = slot + same * (dslot[i] + 1)
        table[p] = jnp.minimum(block, 15)
        table[32 + p] = there
        table[64 + p] = slot

    pl.semaphore_wait(barrier, 34)

    quarter = pl.ds(pl.multiple_of(rep * 512, 512), 512)
    gb = []
    for k in range(1, 4):
        part = w.at[y * 4 + x, c, :, quarter]
        gb.append(copy(part, part, gbs.at[0, k - 1], gbr.at[0, k - 1], at_b(k)))
        gb[-1].start()

    ctok.wait()
    ccot.start()
    cmom.start()
    sends = [None]
    arr0[0] = tok[table[me]]
    metacopies = []
    ga = []
    gz = []
    gc = []
    for j in range(1, 32):
        if j > WINDOW:
            sends[j - WINDOW].wait_send()
        p = peer(MOVES[j])
        spot = stage.at[(j - 1) % WINDOW]
        spot[...] = tok[table[p]]
        cp = copy(spot, landing(j), tss.at[j], tsr.at[j], (p, rep))
        cp.start()
        sends.append(cp)
        if j == 4:
            for cp in gb:
                cp.wait()
            for k in range(1, 4):
                for bb in range(4):
                    part = w.at[place(a, bb), c, :, quarter]
                    ga.append(copy(part, part, gas.at[0, k - 1, bb], gar.at[0, k - 1, bb], at_a(k)))
                    ga[-1].start()
        if j == 6:
            for r in range(4):
                ids = segments[r : r + 1, :]
                live = lax.broadcasted_iota(jnp.int32, (1, 512), 1) < counts[r]
                found = jnp.zeros((1, 512), jnp.int32)
                for v in range(8):
                    hit = jnp.where((ids == v) & live, 1, 0)
                    found = found + hit * jnp.sum(hit, axis=1, keepdims=True)
                for i in range(4):
                    lengths[r * 4 + i] = jnp.broadcast_to(
                        found[:, i * 128 : (i + 1) * 128], (8, 128)
                    )
            line = lax.broadcasted_iota(jnp.int32, (8, 128), 0)
            for n in range(32):
                p = peer(MOVES[n])
                lens = lengths[table[p]] * table[32 + p]
                value = jnp.where(line == 0, lens, table[64 + p])
                if n == 0:
                    metar[0] = value
                else:
                    metasent[n] = value
                    metacopies.append(
                        copy(metasent.at[n], metar.at[n], mss.at[n], msr.at[n], (p, rep))
                    )
                    metacopies[-1].start()
        if j == 10:
            for cp in ga:
                cp.wait()
            for k in range(1, 4):
                part = w.at[:, c, :, quarter]
                gz.append(copy(part, part, gzs.at[k - 1], gzr.at[k - 1], (me, (rep + k) % 4)))
                gz[-1].start()
    for cp in metacopies:
        cp.wait()
    cmeta = pltpu.make_async_copy(metar, metas, lsem.at[3])
    cmeta.start()
    cmom.wait()

    @pl.loop(0, 32)
    def _(i):
        rows = pl.ds(pl.multiple_of(i * 32, 32), 32)
        acc[rows, :] = acc[rows, :] * (momentum_decay / (1.0 - momentum_decay))

    cmeta.wait()
    count = jnp.int32(0)
    for j in range(32):
        count = count + jnp.minimum(metas[j, 1, 0], 1)
        orders[16 + j] = count

    @pl.loop(0, 16)
    def _(k):
        found = jnp.int32(0)
        for j in range(32):
            found = found + jnp.where(orders[16 + j] <= k, 1, 0)
        orders[k] = found

    ccot.wait()
    for cp in gz:
        cp.wait()
    part = w.at[:, c]
    cp = copy(part, part, gcs.at[0, 0], gcr.at[0, 0], other)
    cp.start()
    cp.wait()
    done = 0
    arrived = 1
    blocks = 2
    for number in range(BUFFERS):
        needed = EDGES[number + 1]
        while arrived < needed:
            sends[arrived].wait_recv()
            arrived += 1
        rowcount = blocks * 128
        slots = []
        for i in range(blocks):
            o = jnp.minimum(orders[done + i], 31)
            slots.append(jnp.clip(metas[o, 1, 0] - 1, 0, 15))
            block = arrs[0][jnp.minimum(o, EDGES[1] - 1)]
            for n in range(1, number + 1):
                at = jnp.clip(o - EDGES[n], 0, EDGES[n + 1] - EDGES[n] - 1)
                block = lax.select(o >= EDGES[n], arrs[n][at], block)
            xs[i * 128 : (i + 1) * 128, :] = block
            xt[:, i * 128 : (i + 1) * 128] = jnp.transpose(block)
            lens = metar[o][0:1, :]
            weight = jnp.where(lens > 0, 1.0 / jnp.maximum(lens, 1).astype(F32), 0.0)
            wt[i * 128 : (i + 1) * 128, :] = jnp.transpose(jnp.broadcast_to(weight, (128, 128)))
        done += blocks

        @pl.loop(0, 2048 // TILE)
        def _(n):
            cols = pl.ds(pl.multiple_of(n * TILE, TILE), TILE)
            pre = jnp.dot(
                xs[0:rowcount, :], w[:, :, :, cols].reshape(1024, TILE), preferred_element_type=F32
            )
            parts = []
            for i in range(blocks):
                rows = slice(i * 128, (i + 1) * 128)
                wide = jnp.concatenate([wt[rows, :]] * (TILE // 128), axis=1)
                ci = cot[slots[i], :, cols].astype(F32)
                parts.append((ci * gelu_slope(pre[rows]) * wide).astype(BF16))
            delta = jnp.concatenate(parts, axis=0)
            acc[:, cols] += jnp.dot(xt[:, 0:rowcount], delta, preferred_element_type=F32)

    for j in range(32 - WINDOW, 32):
        sends[j].wait_send()

    def squeezed(yx, core):
        rows = pl.ds(pl.multiple_of((yx * 2 + core) * 32, 32), 32)
        moment = acc[rows, :] * (1.0 - momentum_decay)
        scale = jnp.sum(jnp.abs(moment), axis=1, keepdims=True) * (1.0 / 2048)
        unit = jnp.tanh(moment * (1.0 / (scale + epsilon)))
        return scale.astype(BF16).astype(F32) * unit.astype(BF16).astype(F32)

    @pl.loop(0, 16)
    def _(i):
        yx = place((a + 1 + i // 4) % 4, i % 4)
        u[i] = squeezed(yx, 1 - c).astype(BF16)
        copy(u.at[i], r1.at[yx], c1s.at[i], c1r.at[yx], other).start()

    def add_core(k):
        @pl.loop(0, 4)
        def _(bb):
            yx = place((a + k) % 4, bb)
            copy(u.at[0], r1.at[yx], c1s.at[0], c1r.at[yx], other).wait_recv()
            s1[k, bb] = (squeezed(yx, c) + r1[yx].astype(F32)).astype(BF16)

    stage2 = []
    for k in (2, 1, 3, 0):
        add_core(k)
        if k:
            cp = copy(s1.at[k], r2.at[k - 1], c2s.at[k - 1], c2r.at[k - 1], at_a(k))
            cp.start()
            stage2.append(cp)
    for cp in stage2:
        cp.wait()

    def add_a(bi):
        total = s1[0, bi].astype(F32)
        for k in range(3):
            total = total + r2[k, bi].astype(F32)
        return total

    stage3 = []
    for k in (2, 1, 3):
        s2[k - 1] = add_a((b + k) % 4).astype(BF16)
        cp = copy(s2.at[k - 1], r3.at[k - 1], c3s.at[k - 1], c3r.at[k - 1], at_b(k))
        cp.start()
        stage3.append(cp)
    total = add_a(b)
    for cp in stage3:
        cp.wait()
    for k in range(3):
        total = total + r3[k].astype(F32)
    r4[rep] = total.astype(BF16)
    stage4 = []
    for k in (2, 1, 3):
        cp = copy(r4.at[rep], r4.at[rep], c4s.at[k - 1], c4r.at[k - 1], (me, (rep + k) % 4))
        cp.start()
        stage4.append(cp)
    for cp in stage4:
        cp.wait()
    average = (
        r4[0].astype(F32) + r4[1].astype(F32) + r4[2].astype(F32) + r4[3].astype(F32)
    ) * (1.0 / 128)
    scale = jnp.sum(jnp.abs(average), axis=1, keepdims=True) * (1.0 / 2048)
    moment = scale * jnp.tanh(average / (scale + epsilon))
    out_m[...] = moment
    direction = moment / (jnp.sqrt(variance[...]) + epsilon)
    gathered[y * 4 + x, c] = direction.astype(BF16)

    def group(ai, bi):
        return gathered.at[place(ai, bi), c]

    dcopies = []

    def to_a(bi):
        for k in (2, 1, 3):
            cp = copy(group(a, bi), group(a, bi), gas.at[1, k - 1, bi], gar.at[1, k - 1, bi], at_a(k))
            cp.start()
            dcopies.append(cp)

    def to_core(ai, bi):
        yx = place(ai, bi)
        copy(gathered.at[yx, c], gathered.at[yx, c], gcs.at[1, yx], gcr.at[1, yx], other).start()

    gb = {}
    for k in (2, 1, 3):
        gb[k] = copy(group(a, b), group(a, b), gbs.at[1, k - 1], gbr.at[1, k - 1], at_b(k))
        gb[k].start()
    to_a(b)

    def folded(v):
        line = jnp.sum(v, axis=0, keepdims=True)
        out = line[:, 0:128]
        for i in range(1, 16):
            out = out + line[:, i * 128 : (i + 1) * 128]
        return out

    q[me] = jnp.concatenate(
        [
            folded(master[...] * master[...]),
            folded(direction * direction),
            jnp.zeros((6, 128), F32),
        ],
        axis=0,
    )
    out_l[...] = direction
    scalars = []
    for j in range(1, 32):
        cp = copy(q.at[me], q.at[me], qs.at[j], qr.at[j], (peer(MOVES[j]), rep))
        cp.start()
        scalars.append(cp)

    to_core(a, b)
    for k in (1, 3, 2):
        gb[k].wait()
        to_a((b - k + 4) % 4)
        to_core(a, (b - k + 4) % 4)
    for cp in scalars:
        cp.wait()
    sums = jnp.sum(jnp.sum(q[...], axis=0), axis=1, keepdims=True)
    roots = jnp.sqrt(sums)
    ratio = roots[0:1, :] / (roots[1:2, :] + epsilon)
    out_l[...] = out_l[...] * ratio
    factor = learn_rate * ratio

    def update(yx, core):
        new = w[yx, core].astype(F32) - factor * gathered[yx, core].astype(F32)
        w[yx, core] = new.astype(BF16)
        at = yx * 2 + core
        pltpu.make_async_copy(w.at[yx, core], out_w.at[yx, core], outsem.at[at]).start()

    @pl.loop(0, 4)
    def _(i):
        update(place(a, i), c)

    for k in (1, 3, 2):
        ai = (a - k + 4) % 4

        @pl.loop(0, 4)
        def _(i):
            bi = (b + i) % 4
            copy(
                group(ai, bi), group(ai, bi), gas.at[1, k - 1, bi], gar.at[1, k - 1, bi], at_a(k)
            ).wait_recv()
            to_core(ai, bi)
            update(place(ai, bi), c)

    @pl.loop(0, 16)
    def _(i):
        theirs = gathered.at[i, 1 - c]
        copy(theirs, theirs, gcs.at[1, i], gcr.at[1, i], other).wait_recv()
        update(i, 1 - c)

    for cp in dcopies:
        cp.wait_send()

    @pl.loop(0, 16)
    def _(i):
        mine = gathered.at[i, c]
        copy(mine, mine, gcs.at[1, i], gcr.at[1, i], other).wait_send()
        copy(u.at[i], r1.at[i], c1s.at[i], c1r.at[i], other).wait_send()
        for core in range(2):
            pltpu.make_async_copy(
                w.at[i, core], out_w.at[i, core], outsem.at[i * 2 + core]
            ).wait()


def run(counts, dest, dslot, segments, tokens, cotangent, master, momentum, variance):
    sem = pltpu.SemaphoreType.DMA
    vmem = pl.BlockSpec(memory_space=pltpu.VMEM)
    smem = pl.BlockSpec(memory_space=pltpu.SMEM)
    hbm = pl.BlockSpec(memory_space=pl.ANY)
    return pl.pallas_call(
        kernel,
        out_shape=(
            jax.ShapeDtypeStruct((16, 2, 32, 2048), BF16),
            jax.ShapeDtypeStruct((32, 2048), F32),
            jax.ShapeDtypeStruct((32, 2048), F32),
        ),
        in_specs=[
            smem,
            smem,
            smem,
            vmem,
            hbm,
            hbm,
            vmem,
            hbm,
            vmem,
        ],
        out_specs=(hbm, vmem, vmem),
        scratch_shapes=[
            pltpu.VMEM((16, 128, 1024), BF16),
            pltpu.VMEM((WINDOW, 128, 1024), BF16),
            pltpu.VMEM((18, 128, 1024), BF16),
            pltpu.VMEM((2, 128, 1024), BF16),
            pltpu.VMEM((2, 128, 1024), BF16),
            pltpu.VMEM((2, 128, 1024), BF16),
            pltpu.VMEM((2, 128, 1024), BF16),
            pltpu.VMEM((2, 128, 1024), BF16),
            pltpu.VMEM((2, 128, 1024), BF16),
            pltpu.VMEM((2, 128, 1024), BF16),
            pltpu.VMEM((16, 128, 2048), BF16),
            pltpu.VMEM((16, 2, 32, 2048), BF16),
            pltpu.VMEM((16, 2, 32, 2048), BF16),
            pltpu.VMEM((1024, 2048), F32),
            pltpu.VMEM((256, 1024), BF16),
            pltpu.VMEM((1024, 256), BF16),
            pltpu.VMEM((256, 128), F32),
            pltpu.VMEM((32, 8, 128), jnp.int32),
            pltpu.SMEM((32, 8, 128), jnp.int32),
            pltpu.SMEM((48,), jnp.int32),
            pltpu.SMEM((96,), jnp.int32),
            pltpu.VMEM((16, 8, 128), jnp.int32),
            pltpu.VMEM((32, 8, 128), jnp.int32),
            pltpu.VMEM((16, 32, 2048), BF16),
            pltpu.VMEM((16, 32, 2048), BF16),
            pltpu.VMEM((4, 4, 32, 2048), BF16),
            pltpu.VMEM((3, 4, 32, 2048), BF16),
            pltpu.VMEM((3, 32, 2048), BF16),
            pltpu.VMEM((3, 32, 2048), BF16),
            pltpu.VMEM((4, 32, 2048), BF16),
            pltpu.VMEM((32, 8, 128), F32),
            sem((4,)),
            sem((32,)),
            sem((32,)),
            sem((32,)),
            sem((32,)),
            sem((32,)),
            sem((2, 3)),
            sem((2, 3)),
            sem((2, 3, 4)),
            sem((2, 3, 4)),
            sem((3,)),
            sem((3,)),
            sem((2, 16)),
            sem((2, 16)),
            sem((16,)),
            sem((16,)),
            sem((3,)),
            sem((3,)),
            sem((3,)),
            sem((3,)),
            sem((3,)),
            sem((3,)),
            sem((32,)),
            sem((32,)),
        ],
        compiler_params=pltpu.CompilerParams(
            collective_id=1, has_side_effects=True, vmem_limit_bytes=63 * 2**20
        ),
        cost_estimate=pl.CostEstimate(
            flops=18 * 10**9, bytes_accessed=40 * 10**6, transcendentals=20 * 10**6
        ),
    )(counts, dest, dslot, segments, tokens, cotangent, master, momentum, variance)


def settle(w_in, m_in, l_in, w_out, m_out, l_out):
    w_out[...] = w_in[...]
    m_out[...] = m_in[...]
    l_out[...] = l_in[...]


def per_device(
    tokens,
    token_counts,
    segment_ids,
    dest_device,
    dest_slot,
    cotangent,
    master_weight,
    momentum,
    variance,
):
    new_w, new_m, step = run(
        token_counts,
        dest_device,
        dest_slot,
        segment_ids,
        tokens.reshape(16, 128, 1024),
        cotangent.reshape(16, 128, 2048),
        master_weight,
        momentum,
        variance,
    )
    specs = [pl.BlockSpec((rows, 2048), lambda i: (i, 0)) for rows in (256, 8, 8)]
    return pl.pallas_call(
        settle,
        grid=(4,),
        out_shape=(
            jax.ShapeDtypeStruct((1024, 2048), BF16),
            jax.ShapeDtypeStruct((32, 2048), F32),
            jax.ShapeDtypeStruct((32, 2048), F32),
        ),
        in_specs=specs,
        out_specs=tuple(specs),
        cost_estimate=pl.CostEstimate(flops=0, bytes_accessed=9 * 10**6, transcendentals=0),
    )(new_w.reshape(1024, 2048), new_m, step)


def solution(mesh):
    return jax.shard_map(
        per_device,
        mesh=mesh,
        in_specs=(
            P(("dp", "rep"), None, None),
            P(("dp", "rep")),
            P(("dp", "rep"), None),
            P(("dp", "rep")),
            P(("dp", "rep")),
            P(("dp", "rep"), None),
            P("dp", None),
            P(),
            P("dp", None),
        ),
        out_specs=(P(), P("dp", None), P("dp", None)),
        check_vma=False,
    )
```

```python
import functools

import jax
import jax.numpy as jnp
from jax import lax
from jax.experimental import pallas as pl
from jax.experimental.pallas import tpu as pltpu
from jax.sharding import PartitionSpec as P

MESH = pl.DeviceIdType.MESH
F32 = jnp.float32
BF16 = jnp.bfloat16
momentum_decay = 0.9
learn_rate = 0.05
epsilon = 1e-06
normal_peak = 0.3989422804014327

GROUPS = (
    ((1, 1), (3, 3)),
    ((1, 2), (3, 0)),
    ((2, 1), (0, 3)),
    ((1, 3), (3, 1)),
    ((3, 2), (1, 0)),
    ((2, 3), (0, 1)),
    ((0, 2), (2, 0)),
    ((2, 2),),
)
MOVES = [(0, 0, 0), (0, 0, 1)]
for group in GROUPS:
    for core in (0, 1):
        for dy, dx in group:
            MOVES.append((dy, dx, core))

EDGES = (0, 18, 20, 22, 24, 26, 28, 30, 32)
BUFFERS = len(EDGES) - 1
WINDOW = 8
AHEAD = 6
TILE = 1024


def gelu_slope(a):
    u = jnp.abs(a)
    d = 1.0 + u * (0.3275911 * 0.7071067811865476)
    t = pl.reciprocal(d, approx=True)
    t = t * (2.0 - d * t)
    e = jnp.exp2((a * a) * (-0.5 * 1.4426950408889634))
    poly = t * (
        0.5 * 0.254829592
        + t
        * (
            0.5 * -0.284496736
            + t * (0.5 * 1.421413741 + t * (0.5 * -1.453152027 + t * (0.5 * 1.061405429)))
        )
    )
    h = e * (poly - normal_peak * u)
    return jnp.where(a >= 0.0, 1.0 - h, h)


def kernel(
    counts,
    dest,
    dslot,
    segments,
    tok_hbm,
    cot_hbm,
    master,
    mom_hbm,
    variance,
    out_w,
    out_m,
    out_l,
    tok,
    stage,
    arr0,
    arr1,
    arr2,
    arr3,
    arr4,
    arr5,
    arr6,
    arr7,
    cot,
    w,
    gathered,
    acc,
    xs,
    xt,
    wt,
    metar,
    metas,
    orders,
    table,
    lengths,
    metasent,
    u,
    r1,
    s1,
    r2,
    s2,
    r3,
    r4,
    q,
    lsem,
    outsem,
    tss,
    tsr,
    mss,
    msr,
    gbs,
    gbr,
    gas,
    gar,
    gzs,
    gzr,
    gcs,
    gcr,
    c1s,
    c1r,
    c2s,
    c2r,
    c3s,
    c3r,
    c4s,
    c4r,
    qs,
    qr,
):
    me = lax.axis_index("dp")
    rep = lax.axis_index("rep")
    y = me // 8
    x = (me // 2) % 4
    c = me % 2
    a = (1 - c) * y + c * x
    b = (1 - c) * x + c * y
    sa = 4 * (1 - c) + c
    sb = 4 * c + (1 - c)
    arrs = (arr0, arr1, arr2, arr3, arr4, arr5, arr6, arr7)

    def place(ai, bi):
        return ai * sa + bi * sb

    def at_a(k):
        return (place((a + k) % 4, b) * 2 + c, rep)

    def at_b(k):
        return (place(a, (b + k) % 4) * 2 + c, rep)

    other = (y * 8 + x * 2 + 1 - c, rep)

    def copy(src, dst, ss, rs, dev):
        return pltpu.make_async_remote_copy(
            src_ref=src, dst_ref=dst, send_sem=ss, recv_sem=rs, device_id=dev, device_id_type=MESH
        )

    def peer(move):
        dy, dx, dc = move
        return (((y + dy) % 4) * 4 + (x + dx) % 4) * 2 + (c + dc) % 2

    def landing(j):
        n = max(i for i in range(BUFFERS) if EDGES[i] <= j)
        return arrs[n].at[j - EDGES[n]]

    ctok = pltpu.make_async_copy(tok_hbm, tok, lsem.at[0])
    ccot = pltpu.make_async_copy(cot_hbm, cot, lsem.at[1])
    cmom = pltpu.make_async_copy(mom_hbm, acc, lsem.at[2])
    ctok.start()

    w[y * 4 + x, c] = master[...].astype(BF16)
    barrier = pltpu.get_barrier_semaphore()

    @pl.loop(1, 32)
    def _(k):
        pl.semaphore_signal(barrier, inc=1, device_id=((me + k) % 32, rep), device_id_type=MESH)

    for k in range(1, 4):
        pl.semaphore_signal(barrier, inc=1, device_id=(me, (rep + k) % 4), device_id_type=MESH)

    @pl.loop(0, 32)
    def _(p):
        block, there, slot = jnp.int32(0), jnp.int32(0), jnp.int32(0)
        for i in range(16):
            same = jnp.where(dest[i] == p, 1, 0)
            block = block + same * i
            there = there + same
            slot = slot + same * (dslot[i] + 1)
        table[p] = jnp.minimum(block, 15)
        table[32 + p] = there
        table[64 + p] = slot

    pl.semaphore_wait(barrier, 34)

    quarter = pl.ds(pl.multiple_of(rep * 512, 512), 512)
    gb = []
    for k in range(1, 4):
        part = w.at[y * 4 + x, c, :, quarter]
        gb.append(copy(part, part, gbs.at[0, k - 1], gbr.at[0, k - 1], at_b(k)))
        gb[-1].start()

    ctok.wait()
    ccot.start()
    cmom.start()
    sends = [None]
    arr0[0] = tok[table[me]]
    metacopies = []
    ga = []
    gz = []
    gc = []

    def send(j):
        if j > WINDOW:
            sends[j - WINDOW].wait_send()
        p = peer(MOVES[j])
        spot = stage.at[(j - 1) % WINDOW]
        spot[...] = tok[table[p]]
        cp = copy(spot, landing(j), tss.at[j], tsr.at[j], (p, rep))
        cp.start()
        sends.append(cp)

    for j in range(1, EDGES[1] + AHEAD):
        send(j)
        if j == 4:
            for cp in gb:
                cp.wait()
            for k in range(1, 4):
                for bb in range(4):
                    part = w.at[place(a, bb), c, :, quarter]
                    ga.append(copy(part, part, gas.at[0, k - 1, bb], gar.at[0, k - 1, bb], at_a(k)))
                    ga[-1].start()
        if j == 6:
            for r in range(4):
                ids = segments[r : r + 1, :]
                live = lax.broadcasted_iota(jnp.int32, (1, 512), 1) < counts[r]
                found = jnp.zeros((1, 512), jnp.int32)
                for v in range(8):
                    hit = jnp.where((ids == v) & live, 1, 0)
                    found = found + hit * jnp.sum(hit, axis=1, keepdims=True)
                for i in range(4):
                    lengths[r * 4 + i] = jnp.broadcast_to(
                        found[:, i * 128 : (i + 1) * 128], (8, 128)
                    )
            line = lax.broadcasted_iota(jnp.int32, (8, 128), 0)
            for n in range(32):
                p = peer(MOVES[n])
                lens = lengths[table[p]] * table[32 + p]
                value = jnp.where(line == 0, lens, table[64 + p])
                if n == 0:
                    metar[0] = value
                else:
                    metasent[n] = value
                    metacopies.append(
                        copy(metasent.at[n], metar.at[n], mss.at[n], msr.at[n], (p, rep))
                    )
                    metacopies[-1].start()
        if j == 10:
            for cp in ga:
                cp.wait()
            for k in range(1, 4):
                part = w.at[:, c, :, quarter]
                gz.append(copy(part, part, gzs.at[k - 1], gzr.at[k - 1], (me, (rep + k) % 4)))
                gz[-1].start()
    for cp in metacopies:
        cp.wait()
    cmeta = pltpu.make_async_copy(metar, metas, lsem.at[3])
    cmeta.start()
    cmom.wait()

    @pl.loop(0, 32)
    def _(i):
        rows = pl.ds(pl.multiple_of(i * 32, 32), 32)
        acc[rows, :] = acc[rows, :] * (momentum_decay / (1.0 - momentum_decay))

    cmeta.wait()
    count = jnp.int32(0)
    for j in range(32):
        count = count + jnp.minimum(metas[j, 1, 0], 1)
        orders[16 + j] = count

    @pl.loop(0, 16)
    def _(k):
        found = jnp.int32(0)
        for j in range(32):
            found = found + jnp.where(orders[16 + j] <= k, 1, 0)
        orders[k] = found

    ccot.wait()
    for cp in gz:
        cp.wait()
    part = w.at[:, c]
    cp = copy(part, part, gcs.at[0, 0], gcr.at[0, 0], other)
    cp.start()
    cp.wait()
    done = 0
    arrived = 1
    blocks = 2
    for number in range(BUFFERS):
        needed = EDGES[number + 1]
        while len(sends) < min(needed + AHEAD, 32):
            send(len(sends))
        while arrived < needed:
            sends[arrived].wait_recv()
            arrived += 1
        rowcount = blocks * 128
        slots = []
        for i in range(blocks):
            o = jnp.minimum(orders[done + i], 31)
            slots.append(jnp.clip(metas[o, 1, 0] - 1, 0, 15))
            block = arrs[0][jnp.minimum(o, EDGES[1] - 1)]
            for n in range(1, number + 1):
                at = jnp.clip(o - EDGES[n], 0, EDGES[n + 1] - EDGES[n] - 1)
                block = lax.select(o >= EDGES[n], arrs[n][at], block)
            xs[i * 128 : (i + 1) * 128, :] = block
            xt[:, i * 128 : (i + 1) * 128] = jnp.transpose(block)
            lens = metar[o][0:1, :]
            weight = jnp.where(lens > 0, 1.0 / jnp.maximum(lens, 1).astype(F32), 0.0)
            wt[i * 128 : (i + 1) * 128, :] = jnp.transpose(jnp.broadcast_to(weight, (128, 128)))
        done += blocks

        @pl.loop(0, 2048 // TILE)
        def _(n):
            cols = pl.ds(pl.multiple_of(n * TILE, TILE), TILE)
            pre = jnp.dot(
                xs[0:rowcount, :], w[:, :, :, cols].reshape(1024, TILE), preferred_element_type=F32
            )
            parts = []
            for i in range(blocks):
                rows = slice(i * 128, (i + 1) * 128)
                wide = jnp.concatenate([wt[rows, :]] * (TILE // 128), axis=1)
                ci = cot[slots[i], :, cols].astype(F32)
                parts.append((ci * gelu_slope(pre[rows]) * wide).astype(BF16))
            delta = jnp.concatenate(parts, axis=0)
            acc[:, cols] += jnp.dot(xt[:, 0:rowcount], delta, preferred_element_type=F32)

    for j in range(32 - WINDOW, 32):
        sends[j].wait_send()

    def squeezed(yx, core):
        rows = pl.ds(pl.multiple_of((yx * 2 + core) * 32, 32), 32)
        moment = acc[rows, :] * (1.0 - momentum_decay)
        scale = jnp.sum(jnp.abs(moment), axis=1, keepdims=True) * (1.0 / 2048)
        unit = jnp.tanh(moment * (1.0 / (scale + epsilon)))
        return scale.astype(BF16).astype(F32) * unit.astype(BF16).astype(F32)

    @pl.loop(0, 16)
    def _(i):
        yx = place((a + 1 + i // 4) % 4, i % 4)
        u[i] = squeezed(yx, 1 - c).astype(BF16)
        copy(u.at[i], r1.at[yx], c1s.at[i], c1r.at[yx], other).start()

    def add_core(k):
        @pl.loop(0, 4)
        def _(bb):
            yx = place((a + k) % 4, bb)
            copy(u.at[0], r1.at[yx], c1s.at[0], c1r.at[yx], other).wait_recv()
            s1[k, bb] = (squeezed(yx, c) + r1[yx].astype(F32)).astype(BF16)

    stage2 = []
    for k in (2, 1, 3, 0):
        add_core(k)
        if k:
            cp = copy(s1.at[k], r2.at[k - 1], c2s.at[k - 1], c2r.at[k - 1], at_a(k))
            cp.start()
            stage2.append(cp)
    for cp in stage2:
        cp.wait()

    def add_a(bi):
        total = s1[0, bi].astype(F32)
        for k in range(3):
            total = total + r2[k, bi].astype(F32)
        return total

    stage3 = []
    for k in (2, 1, 3):
        s2[k - 1] = add_a((b + k) % 4).astype(BF16)
        cp = copy(s2.at[k - 1], r3.at[k - 1], c3s.at[k - 1], c3r.at[k - 1], at_b(k))
        cp.start()
        stage3.append(cp)
    total = add_a(b)
    for cp in stage3:
        cp.wait()
    for k in range(3):
        total = total + r3[k].astype(F32)
    r4[rep] = total.astype(BF16)
    stage4 = []
    for k in (2, 1, 3):
        cp = copy(r4.at[rep], r4.at[rep], c4s.at[k - 1], c4r.at[k - 1], (me, (rep + k) % 4))
        cp.start()
        stage4.append(cp)
    for cp in stage4:
        cp.wait()
    average = (
        r4[0].astype(F32) + r4[1].astype(F32) + r4[2].astype(F32) + r4[3].astype(F32)
    ) * (1.0 / 128)
    scale = jnp.sum(jnp.abs(average), axis=1, keepdims=True) * (1.0 / 2048)
    moment = scale * jnp.tanh(average / (scale + epsilon))
    out_m[...] = moment
    direction = moment / (jnp.sqrt(variance[...]) + epsilon)
    gathered[y * 4 + x, c] = direction.astype(BF16)

    def group(ai, bi):
        return gathered.at[place(ai, bi), c]

    dcopies = []

    def to_a(bi):
        for k in (2, 1, 3):
            cp = copy(group(a, bi), group(a, bi), gas.at[1, k - 1, bi], gar.at[1, k - 1, bi], at_a(k))
            cp.start()
            dcopies.append(cp)

    def to_core(ai, bi):
        yx = place(ai, bi)
        copy(gathered.at[yx, c], gathered.at[yx, c], gcs.at[1, yx], gcr.at[1, yx], other).start()

    gb = {}
    for k in (2, 1, 3):
        gb[k] = copy(group(a, b), group(a, b), gbs.at[1, k - 1], gbr.at[1, k - 1], at_b(k))
        gb[k].start()
    to_a(b)

    def folded(v):
        line = jnp.sum(v, axis=0, keepdims=True)
        out = line[:, 0:128]
        for i in range(1, 16):
            out = out + line[:, i * 128 : (i + 1) * 128]
        return out

    q[me] = jnp.concatenate(
        [
            folded(master[...] * master[...]),
            folded(direction * direction),
            jnp.zeros((6, 128), F32),
        ],
        axis=0,
    )
    out_l[...] = direction
    scalars = []
    for j in range(1, 32):
        cp = copy(q.at[me], q.at[me], qs.at[j], qr.at[j], (peer(MOVES[j]), rep))
        cp.start()
        scalars.append(cp)

    to_core(a, b)
    for k in (1, 3, 2):
        gb[k].wait()
        to_a((b - k + 4) % 4)
        to_core(a, (b - k + 4) % 4)
    for cp in scalars:
        cp.wait()
    sums = jnp.sum(jnp.sum(q[...], axis=0), axis=1, keepdims=True)
    roots = jnp.sqrt(sums)
    ratio = roots[0:1, :] / (roots[1:2, :] + epsilon)
    out_l[...] = out_l[...] * ratio
    factor = learn_rate * ratio

    def update(yx, core):
        new = w[yx, core].astype(F32) - factor * gathered[yx, core].astype(F32)
        w[yx, core] = new.astype(BF16)
        at = yx * 2 + core
        pltpu.make_async_copy(w.at[yx, core], out_w.at[yx, core], outsem.at[at]).start()

    @pl.loop(0, 4)
    def _(i):
        update(place(a, i), c)

    for k in (1, 3, 2):
        ai = (a - k + 4) % 4

        @pl.loop(0, 4)
        def _(i):
            bi = (b + i) % 4
            copy(
                group(ai, bi), group(ai, bi), gas.at[1, k - 1, bi], gar.at[1, k - 1, bi], at_a(k)
            ).wait_recv()
            to_core(ai, bi)
            update(place(ai, bi), c)

    @pl.loop(0, 16)
    def _(i):
        theirs = gathered.at[i, 1 - c]
        copy(theirs, theirs, gcs.at[1, i], gcr.at[1, i], other).wait_recv()
        update(i, 1 - c)

    for cp in dcopies:
        cp.wait_send()

    @pl.loop(0, 16)
    def _(i):
        mine = gathered.at[i, c]
        copy(mine, mine, gcs.at[1, i], gcr.at[1, i], other).wait_send()
        copy(u.at[i], r1.at[i], c1s.at[i], c1r.at[i], other).wait_send()
        for core in range(2):
            pltpu.make_async_copy(
                w.at[i, core], out_w.at[i, core], outsem.at[i * 2 + core]
            ).wait()


def run(counts, dest, dslot, segments, tokens, cotangent, master, momentum, variance):
    sem = pltpu.SemaphoreType.DMA
    vmem = pl.BlockSpec(memory_space=pltpu.VMEM)
    smem = pl.BlockSpec(memory_space=pltpu.SMEM)
    hbm = pl.BlockSpec(memory_space=pl.ANY)
    return pl.pallas_call(
        kernel,
        out_shape=(
            jax.ShapeDtypeStruct((16, 2, 32, 2048), BF16),
            jax.ShapeDtypeStruct((32, 2048), F32),
            jax.ShapeDtypeStruct((32, 2048), F32),
        ),
        in_specs=[
            smem,
            smem,
            smem,
            vmem,
            hbm,
            hbm,
            vmem,
            hbm,
            vmem,
        ],
        out_specs=(hbm, vmem, vmem),
        scratch_shapes=[
            pltpu.VMEM((16, 128, 1024), BF16),
            pltpu.VMEM((WINDOW, 128, 1024), BF16),
            pltpu.VMEM((18, 128, 1024), BF16),
            pltpu.VMEM((2, 128, 1024), BF16),
            pltpu.VMEM((2, 128, 1024), BF16),
            pltpu.VMEM((2, 128, 1024), BF16),
            pltpu.VMEM((2, 128, 1024), BF16),
            pltpu.VMEM((2, 128, 1024), BF16),
            pltpu.VMEM((2, 128, 1024), BF16),
            pltpu.VMEM((2, 128, 1024), BF16),
            pltpu.VMEM((16, 128, 2048), BF16),
            pltpu.VMEM((16, 2, 32, 2048), BF16),
            pltpu.VMEM((16, 2, 32, 2048), BF16),
            pltpu.VMEM((1024, 2048), F32),
            pltpu.VMEM((256, 1024), BF16),
            pltpu.VMEM((1024, 256), BF16),
            pltpu.VMEM((256, 128), F32),
            pltpu.VMEM((32, 8, 128), jnp.int32),
            pltpu.SMEM((32, 8, 128), jnp.int32),
            pltpu.SMEM((48,), jnp.int32),
            pltpu.SMEM((96,), jnp.int32),
            pltpu.VMEM((16, 8, 128), jnp.int32),
            pltpu.VMEM((32, 8, 128), jnp.int32),
            pltpu.VMEM((16, 32, 2048), BF16),
            pltpu.VMEM((16, 32, 2048), BF16),
            pltpu.VMEM((4, 4, 32, 2048), BF16),
            pltpu.VMEM((3, 4, 32, 2048), BF16),
            pltpu.VMEM((3, 32, 2048), BF16),
            pltpu.VMEM((3, 32, 2048), BF16),
            pltpu.VMEM((4, 32, 2048), BF16),
            pltpu.VMEM((32, 8, 128), F32),
            sem((4,)),
            sem((32,)),
            sem((32,)),
            sem((32,)),
            sem((32,)),
            sem((32,)),
            sem((2, 3)),
            sem((2, 3)),
            sem((2, 3, 4)),
            sem((2, 3, 4)),
            sem((3,)),
            sem((3,)),
            sem((2, 16)),
            sem((2, 16)),
            sem((16,)),
            sem((16,)),
            sem((3,)),
            sem((3,)),
            sem((3,)),
            sem((3,)),
            sem((3,)),
            sem((3,)),
            sem((32,)),
            sem((32,)),
        ],
        compiler_params=pltpu.CompilerParams(
            collective_id=1, has_side_effects=True, vmem_limit_bytes=63 * 2**20
        ),
        cost_estimate=pl.CostEstimate(
            flops=18 * 10**9, bytes_accessed=40 * 10**6, transcendentals=20 * 10**6
        ),
    )(counts, dest, dslot, segments, tokens, cotangent, master, momentum, variance)


def settle(w_in, m_in, l_in, w_out, m_out, l_out):
    w_out[...] = w_in[...]
    m_out[...] = m_in[...]
    l_out[...] = l_in[...]


def per_device(
    tokens,
    token_counts,
    segment_ids,
    dest_device,
    dest_slot,
    cotangent,
    master_weight,
    momentum,
    variance,
):
    new_w, new_m, step = run(
        token_counts,
        dest_device,
        dest_slot,
        segment_ids,
        tokens.reshape(16, 128, 1024),
        cotangent.reshape(16, 128, 2048),
        master_weight,
        momentum,
        variance,
    )
    specs = [pl.BlockSpec((rows, 2048), lambda i: (i, 0)) for rows in (256, 8, 8)]
    return pl.pallas_call(
        settle,
        grid=(4,),
        out_shape=(
            jax.ShapeDtypeStruct((1024, 2048), BF16),
            jax.ShapeDtypeStruct((32, 2048), F32),
            jax.ShapeDtypeStruct((32, 2048), F32),
        ),
        in_specs=specs,
        out_specs=tuple(specs),
        cost_estimate=pl.CostEstimate(flops=0, bytes_accessed=9 * 10**6, transcendentals=0),
    )(new_w.reshape(1024, 2048), new_m, step)


def solution(mesh):
    return jax.shard_map(
        per_device,
        mesh=mesh,
        in_specs=(
            P(("dp", "rep"), None, None),
            P(("dp", "rep")),
            P(("dp", "rep"), None),
            P(("dp", "rep")),
            P(("dp", "rep")),
            P(("dp", "rep"), None),
            P("dp", None),
            P(),
            P("dp", None),
        ),
        out_specs=(P(), P("dp", None), P("dp", None)),
        check_vma=False,
    )
```

```python
import functools

import jax
import jax.numpy as jnp
from jax import lax
from jax.experimental import pallas as pl
from jax.experimental.pallas import tpu as pltpu
from jax.sharding import PartitionSpec as P

MESH = pl.DeviceIdType.MESH
F32 = jnp.float32
BF16 = jnp.bfloat16
momentum_decay = 0.9
learn_rate = 0.05
epsilon = 1e-06
normal_peak = 0.3989422804014327

GROUPS = (
    ((1, 1), (3, 3)),
    ((1, 2), (3, 0)),
    ((2, 1), (0, 3)),
    ((1, 3), (3, 1)),
    ((3, 2), (1, 0)),
    ((2, 3), (0, 1)),
    ((0, 2), (2, 0)),
    ((2, 2),),
)
MOVES = [(0, 0, 0), (0, 0, 1)]
for group in GROUPS:
    for core in (0, 1):
        for dy, dx in group:
            MOVES.append((dy, dx, core))

EDGES = (0, 18, 22, 26, 30, 32)
BUFFERS = len(EDGES) - 1
WINDOW = 8
AHEAD = 8
TILE = 1024


def gelu_slope(a):
    u = jnp.abs(a)
    d = 1.0 + u * (0.3275911 * 0.7071067811865476)
    t = pl.reciprocal(d, approx=True)
    t = t * (2.0 - d * t)
    e = jnp.exp2((a * a) * (-0.5 * 1.4426950408889634))
    poly = t * (
        0.5 * 0.254829592
        + t
        * (
            0.5 * -0.284496736
            + t * (0.5 * 1.421413741 + t * (0.5 * -1.453152027 + t * (0.5 * 1.061405429)))
        )
    )
    h = e * (poly - normal_peak * u)
    return jnp.where(a >= 0.0, 1.0 - h, h)


def kernel(
    counts,
    dest,
    dslot,
    segments,
    tok_hbm,
    cot_hbm,
    master,
    mom_hbm,
    variance,
    out_w,
    out_m,
    out_l,
    tok,
    stage,
    arr0,
    arr1,
    arr2,
    arr3,
    arr4,
    cot,
    w,
    gathered,
    acc,
    xs,
    xt,
    wt,
    metar,
    metas,
    orders,
    table,
    lengths,
    metasent,
    u,
    r1,
    s1,
    r2,
    s2,
    r3,
    r4,
    q,
    lsem,
    outsem,
    tss,
    tsr,
    mss,
    msr,
    gbs,
    gbr,
    gas,
    gar,
    gzs,
    gzr,
    gcs,
    gcr,
    c1s,
    c1r,
    c2s,
    c2r,
    c3s,
    c3r,
    c4s,
    c4r,
    qs,
    qr,
):
    me = lax.axis_index("dp")
    rep = lax.axis_index("rep")
    y = me // 8
    x = (me // 2) % 4
    c = me % 2
    a = (1 - c) * y + c * x
    b = (1 - c) * x + c * y
    sa = 4 * (1 - c) + c
    sb = 4 * c + (1 - c)
    arrs = (arr0, arr1, arr2, arr3, arr4)

    def place(ai, bi):
        return ai * sa + bi * sb

    def at_a(k):
        return (place((a + k) % 4, b) * 2 + c, rep)

    def at_b(k):
        return (place(a, (b + k) % 4) * 2 + c, rep)

    other = (y * 8 + x * 2 + 1 - c, rep)

    def copy(src, dst, ss, rs, dev):
        return pltpu.make_async_remote_copy(
            src_ref=src, dst_ref=dst, send_sem=ss, recv_sem=rs, device_id=dev, device_id_type=MESH
        )

    def peer(move):
        dy, dx, dc = move
        return (((y + dy) % 4) * 4 + (x + dx) % 4) * 2 + (c + dc) % 2

    def landing(j):
        n = max(i for i in range(BUFFERS) if EDGES[i] <= j)
        return arrs[n].at[j - EDGES[n]]

    ctok = pltpu.make_async_copy(tok_hbm, tok, lsem.at[0])
    ccot = pltpu.make_async_copy(cot_hbm, cot, lsem.at[1])
    cmom = pltpu.make_async_copy(mom_hbm, acc, lsem.at[2])
    ctok.start()

    w[y * 4 + x, c] = master[...].astype(BF16)
    barrier = pltpu.get_barrier_semaphore()

    @pl.loop(1, 32)
    def _(k):
        pl.semaphore_signal(barrier, inc=1, device_id=((me + k) % 32, rep), device_id_type=MESH)

    for k in range(1, 4):
        pl.semaphore_signal(barrier, inc=1, device_id=(me, (rep + k) % 4), device_id_type=MESH)

    @pl.loop(0, 32)
    def _(p):
        block, there, slot = jnp.int32(0), jnp.int32(0), jnp.int32(0)
        for i in range(16):
            same = jnp.where(dest[i] == p, 1, 0)
            block = block + same * i
            there = there + same
            slot = slot + same * (dslot[i] + 1)
        table[p] = jnp.minimum(block, 15)
        table[32 + p] = there
        table[64 + p] = slot

    pl.semaphore_wait(barrier, 34)

    quarter = pl.ds(pl.multiple_of(rep * 512, 512), 512)
    gb = []
    for k in range(1, 4):
        part = w.at[y * 4 + x, c, :, quarter]
        gb.append(copy(part, part, gbs.at[0, k - 1], gbr.at[0, k - 1], at_b(k)))
        gb[-1].start()

    ctok.wait()
    ccot.start()
    cmom.start()
    sends = [None]
    arr0[0] = tok[table[me]]
    metacopies = []
    ga = []
    gz = []
    gc = []

    def send(j):
        if j > WINDOW:
            sends[j - WINDOW].wait_send()
        p = peer(MOVES[j])
        spot = stage.at[(j - 1) % WINDOW]
        spot[...] = tok[table[p]]
        cp = copy(spot, landing(j), tss.at[j], tsr.at[j], (p, rep))
        cp.start()
        sends.append(cp)

    def prepare():
        for cp in metacopies:
            cp.wait()
        cmeta = pltpu.make_async_copy(metar, metas, lsem.at[3])
        cmeta.start()
        cmom.wait()

        @pl.loop(0, 32)
        def _(i):
            rows = pl.ds(pl.multiple_of(i * 32, 32), 32)
            acc[rows, :] = acc[rows, :] * (momentum_decay / (1.0 - momentum_decay))

        cmeta.wait()
        count = jnp.int32(0)
        for j in range(32):
            count = count + jnp.minimum(metas[j, 1, 0], 1)
            orders[16 + j] = count

        @pl.loop(0, 16)
        def _(k):
            found = jnp.int32(0)
            for j in range(32):
                found = found + jnp.where(orders[16 + j] <= k, 1, 0)
            orders[k] = found

        for cp in gz:
            cp.wait()
        part = w.at[:, c]
        gc.append(copy(part, part, gcs.at[0, 0], gcr.at[0, 0], other))
        gc[0].start()

    for j in range(1, EDGES[1] + AHEAD):
        send(j)
        if j == 4:
            for cp in gb:
                cp.wait()
            for k in range(1, 4):
                for bb in range(4):
                    part = w.at[place(a, bb), c, :, quarter]
                    ga.append(copy(part, part, gas.at[0, k - 1, bb], gar.at[0, k - 1, bb], at_a(k)))
                    ga[-1].start()
        if j == 6:
            for r in range(4):
                ids = segments[r : r + 1, :]
                live = lax.broadcasted_iota(jnp.int32, (1, 512), 1) < counts[r]
                found = jnp.zeros((1, 512), jnp.int32)
                for v in range(8):
                    hit = jnp.where((ids == v) & live, 1, 0)
                    found = found + hit * jnp.sum(hit, axis=1, keepdims=True)
                for i in range(4):
                    lengths[r * 4 + i] = jnp.broadcast_to(
                        found[:, i * 128 : (i + 1) * 128], (8, 128)
                    )
            line = lax.broadcasted_iota(jnp.int32, (8, 128), 0)
            for n in range(32):
                p = peer(MOVES[n])
                lens = lengths[table[p]] * table[32 + p]
                value = jnp.where(line == 0, lens, table[64 + p])
                if n == 0:
                    metar[0] = value
                else:
                    metasent[n] = value
                    metacopies.append(
                        copy(metasent.at[n], metar.at[n], mss.at[n], msr.at[n], (p, rep))
                    )
                    metacopies[-1].start()
        if j == 10:
            for cp in ga:
                cp.wait()
            for k in range(1, 4):
                part = w.at[:, c, :, quarter]
                gz.append(copy(part, part, gzs.at[k - 1], gzr.at[k - 1], (me, (rep + k) % 4)))
                gz[-1].start()
        if j == 17:
            prepare()
    ccot.wait()
    gc[0].wait()

    done = 0
    arrived = 1
    for number in range(BUFFERS):
        needed = EDGES[number + 1]
        while len(sends) < min(needed + AHEAD, 32):
            send(len(sends))
        while arrived < needed:
            sends[arrived].wait_recv()
            arrived += 1
        blocks = needed - 16 - done
        rowcount = blocks * 128
        slots = []
        for i in range(blocks):
            o = jnp.minimum(orders[done + i], 31)
            slots.append(jnp.clip(metas[o, 1, 0] - 1, 0, 15))
            block = arrs[0][jnp.minimum(o, EDGES[1] - 1)]
            for n in range(1, number + 1):
                at = jnp.clip(o - EDGES[n], 0, EDGES[n + 1] - EDGES[n] - 1)
                block = lax.select(o >= EDGES[n], arrs[n][at], block)
            xs[i * 128 : (i + 1) * 128, :] = block
            xt[:, i * 128 : (i + 1) * 128] = jnp.transpose(block)
            lens = metar[o][0:1, :]
            weight = jnp.where(lens > 0, 1.0 / jnp.maximum(lens, 1).astype(F32), 0.0)
            wt[i * 128 : (i + 1) * 128, :] = jnp.transpose(jnp.broadcast_to(weight, (128, 128)))
        done += blocks

        @pl.loop(0, 2048 // TILE)
        def _(n):
            cols = pl.ds(pl.multiple_of(n * TILE, TILE), TILE)
            pre = jnp.dot(
                xs[0:rowcount, :], w[:, :, :, cols].reshape(1024, TILE), preferred_element_type=F32
            )
            parts = []
            for i in range(blocks):
                rows = slice(i * 128, (i + 1) * 128)
                wide = jnp.concatenate([wt[rows, :]] * (TILE // 128), axis=1)
                ci = cot[slots[i], :, cols].astype(F32)
                parts.append((ci * gelu_slope(pre[rows]) * wide).astype(BF16))
            delta = jnp.concatenate(parts, axis=0)
            acc[:, cols] += jnp.dot(xt[:, 0:rowcount], delta, preferred_element_type=F32)

    for j in range(32 - WINDOW, 32):
        sends[j].wait_send()

    def squeezed(yx, core):
        rows = pl.ds(pl.multiple_of((yx * 2 + core) * 32, 32), 32)
        moment = acc[rows, :] * (1.0 - momentum_decay)
        scale = jnp.sum(jnp.abs(moment), axis=1, keepdims=True) * (1.0 / 2048)
        unit = jnp.tanh(moment * (1.0 / (scale + epsilon)))
        return scale.astype(BF16).astype(F32) * unit.astype(BF16).astype(F32)

    @pl.loop(0, 16)
    def _(i):
        yx = place((a + 1 + i // 4) % 4, i % 4)
        u[i] = squeezed(yx, 1 - c).astype(BF16)
        copy(u.at[i], r1.at[yx], c1s.at[i], c1r.at[yx], other).start()

    def add_core(k):
        @pl.loop(0, 4)
        def _(bb):
            yx = place((a + k) % 4, bb)
            copy(u.at[0], r1.at[yx], c1s.at[0], c1r.at[yx], other).wait_recv()
            s1[k, bb] = (squeezed(yx, c) + r1[yx].astype(F32)).astype(BF16)

    stage2 = []
    for k in (2, 1, 3, 0):
        add_core(k)
        if k:
            cp = copy(s1.at[k], r2.at[k - 1], c2s.at[k - 1], c2r.at[k - 1], at_a(k))
            cp.start()
            stage2.append(cp)
    for cp in stage2:
        cp.wait()

    def add_a(bi):
        total = s1[0, bi].astype(F32)
        for k in range(3):
            total = total + r2[k, bi].astype(F32)
        return total

    stage3 = []
    for k in (2, 1, 3):
        s2[k - 1] = add_a((b + k) % 4).astype(BF16)
        cp = copy(s2.at[k - 1], r3.at[k - 1], c3s.at[k - 1], c3r.at[k - 1], at_b(k))
        cp.start()
        stage3.append(cp)
    total = add_a(b)
    for cp in stage3:
        cp.wait()
    for k in range(3):
        total = total + r3[k].astype(F32)
    r4[rep] = total.astype(BF16)
    stage4 = []
    for k in (2, 1, 3):
        cp = copy(r4.at[rep], r4.at[rep], c4s.at[k - 1], c4r.at[k - 1], (me, (rep + k) % 4))
        cp.start()
        stage4.append(cp)
    for cp in stage4:
        cp.wait()
    average = (
        r4[0].astype(F32) + r4[1].astype(F32) + r4[2].astype(F32) + r4[3].astype(F32)
    ) * (1.0 / 128)
    scale = jnp.sum(jnp.abs(average), axis=1, keepdims=True) * (1.0 / 2048)
    moment = scale * jnp.tanh(average / (scale + epsilon))
    out_m[...] = moment
    direction = moment / (jnp.sqrt(variance[...]) + epsilon)
    gathered[y * 4 + x, c] = direction.astype(BF16)

    def group(ai, bi):
        return gathered.at[place(ai, bi), c]

    dcopies = []

    def to_a(bi):
        for k in (2, 1, 3):
            cp = copy(group(a, bi), group(a, bi), gas.at[1, k - 1, bi], gar.at[1, k - 1, bi], at_a(k))
            cp.start()
            dcopies.append(cp)

    def to_core(ai, bi):
        yx = place(ai, bi)
        copy(gathered.at[yx, c], gathered.at[yx, c], gcs.at[1, yx], gcr.at[1, yx], other).start()

    gb = {}
    for k in (2, 1, 3):
        gb[k] = copy(group(a, b), group(a, b), gbs.at[1, k - 1], gbr.at[1, k - 1], at_b(k))
        gb[k].start()
    to_a(b)

    def folded(v):
        line = jnp.sum(v, axis=0, keepdims=True)
        out = line[:, 0:128]
        for i in range(1, 16):
            out = out + line[:, i * 128 : (i + 1) * 128]
        return out

    q[me] = jnp.concatenate(
        [
            folded(master[...] * master[...]),
            folded(direction * direction),
            jnp.zeros((6, 128), F32),
        ],
        axis=0,
    )
    out_l[...] = direction
    scalars = []
    for j in range(1, 32):
        cp = copy(q.at[me], q.at[me], qs.at[j], qr.at[j], (peer(MOVES[j]), rep))
        cp.start()
        scalars.append(cp)

    to_core(a, b)
    for k in (1, 3, 2):
        gb[k].wait()
        to_a((b - k + 4) % 4)
        to_core(a, (b - k + 4) % 4)
    for cp in scalars:
        cp.wait()
    sums = jnp.sum(jnp.sum(q[...], axis=0), axis=1, keepdims=True)
    roots = jnp.sqrt(sums)
    ratio = roots[0:1, :] / (roots[1:2, :] + epsilon)
    out_l[...] = out_l[...] * ratio
    factor = learn_rate * ratio

    def update(yx, core):
        new = w[yx, core].astype(F32) - factor * gathered[yx, core].astype(F32)
        w[yx, core] = new.astype(BF16)
        at = yx * 2 + core
        pltpu.make_async_copy(w.at[yx, core], out_w.at[yx, core], outsem.at[at]).start()

    @pl.loop(0, 4)
    def _(i):
        update(place(a, i), c)

    for k in (1, 3, 2):
        ai = (a - k + 4) % 4

        @pl.loop(0, 4)
        def _(i):
            bi = (b + i) % 4
            copy(
                group(ai, bi), group(ai, bi), gas.at[1, k - 1, bi], gar.at[1, k - 1, bi], at_a(k)
            ).wait_recv()
            to_core(ai, bi)
            update(place(ai, bi), c)

    @pl.loop(0, 16)
    def _(i):
        theirs = gathered.at[i, 1 - c]
        copy(theirs, theirs, gcs.at[1, i], gcr.at[1, i], other).wait_recv()
        update(i, 1 - c)

    for cp in dcopies:
        cp.wait_send()

    @pl.loop(0, 16)
    def _(i):
        mine = gathered.at[i, c]
        copy(mine, mine, gcs.at[1, i], gcr.at[1, i], other).wait_send()
        copy(u.at[i], r1.at[i], c1s.at[i], c1r.at[i], other).wait_send()
        for core in range(2):
            pltpu.make_async_copy(
                w.at[i, core], out_w.at[i, core], outsem.at[i * 2 + core]
            ).wait()


def run(counts, dest, dslot, segments, tokens, cotangent, master, momentum, variance):
    sem = pltpu.SemaphoreType.DMA
    vmem = pl.BlockSpec(memory_space=pltpu.VMEM)
    smem = pl.BlockSpec(memory_space=pltpu.SMEM)
    hbm = pl.BlockSpec(memory_space=pl.ANY)
    return pl.pallas_call(
        kernel,
        out_shape=(
            jax.ShapeDtypeStruct((16, 2, 32, 2048), BF16),
            jax.ShapeDtypeStruct((32, 2048), F32),
            jax.ShapeDtypeStruct((32, 2048), F32),
        ),
        in_specs=[
            smem,
            smem,
            smem,
            vmem,
            hbm,
            hbm,
            vmem,
            hbm,
            vmem,
        ],
        out_specs=(hbm, vmem, vmem),
        scratch_shapes=[
            pltpu.VMEM((16, 128, 1024), BF16),
            pltpu.VMEM((WINDOW, 128, 1024), BF16),
            pltpu.VMEM((18, 128, 1024), BF16),
            pltpu.VMEM((4, 128, 1024), BF16),
            pltpu.VMEM((4, 128, 1024), BF16),
            pltpu.VMEM((4, 128, 1024), BF16),
            pltpu.VMEM((2, 128, 1024), BF16),
            pltpu.VMEM((16, 128, 2048), BF16),
            pltpu.VMEM((16, 2, 32, 2048), BF16),
            pltpu.VMEM((16, 2, 32, 2048), BF16),
            pltpu.VMEM((1024, 2048), F32),
            pltpu.VMEM((512, 1024), BF16),
            pltpu.VMEM((1024, 512), BF16),
            pltpu.VMEM((512, 128), F32),
            pltpu.VMEM((32, 8, 128), jnp.int32),
            pltpu.SMEM((32, 8, 128), jnp.int32),
            pltpu.SMEM((48,), jnp.int32),
            pltpu.SMEM((96,), jnp.int32),
            pltpu.VMEM((16, 8, 128), jnp.int32),
            pltpu.VMEM((32, 8, 128), jnp.int32),
            pltpu.VMEM((16, 32, 2048), BF16),
            pltpu.VMEM((16, 32, 2048), BF16),
            pltpu.VMEM((4, 4, 32, 2048), BF16),
            pltpu.VMEM((3, 4, 32, 2048), BF16),
            pltpu.VMEM((3, 32, 2048), BF16),
            pltpu.VMEM((3, 32, 2048), BF16),
            pltpu.VMEM((4, 32, 2048), BF16),
            pltpu.VMEM((32, 8, 128), F32),
            sem((4,)),
            sem((32,)),
            sem((32,)),
            sem((32,)),
            sem((32,)),
            sem((32,)),
            sem((2, 3)),
            sem((2, 3)),
            sem((2, 3, 4)),
            sem((2, 3, 4)),
            sem((3,)),
            sem((3,)),
            sem((2, 16)),
            sem((2, 16)),
            sem((16,)),
            sem((16,)),
            sem((3,)),
            sem((3,)),
            sem((3,)),
            sem((3,)),
            sem((3,)),
            sem((3,)),
            sem((32,)),
            sem((32,)),
        ],
        compiler_params=pltpu.CompilerParams(
            collective_id=1, has_side_effects=True, vmem_limit_bytes=63 * 2**20
        ),
        cost_estimate=pl.CostEstimate(
            flops=18 * 10**9, bytes_accessed=40 * 10**6, transcendentals=20 * 10**6
        ),
    )(counts, dest, dslot, segments, tokens, cotangent, master, momentum, variance)


def settle(w_in, m_in, l_in, w_out, m_out, l_out, w_mid, m_mid, l_mid, in_sem, out_sem):
    moves = []
    for i in range(4):
        rows = pl.ds(i * 256, 256)
        moves.append((w_in.at[rows], w_mid.at[rows], w_out.at[rows]))
    moves.append((m_in, m_mid, m_out))
    moves.append((l_in, l_mid, l_out))
    reads = [pltpu.make_async_copy(s, m, in_sem.at[i]) for i, (s, m, d) in enumerate(moves)]
    writes = [pltpu.make_async_copy(m, d, out_sem.at[i]) for i, (s, m, d) in enumerate(moves)]
    for cp in reads:
        cp.start()
    for read, write in zip(reads, writes):
        read.wait()
        write.start()
    for cp in writes:
        cp.wait()


def per_device(
    tokens,
    token_counts,
    segment_ids,
    dest_device,
    dest_slot,
    cotangent,
    master_weight,
    momentum,
    variance,
):
    new_w, new_m, step = run(
        token_counts,
        dest_device,
        dest_slot,
        segment_ids,
        tokens.reshape(16, 128, 1024),
        cotangent.reshape(16, 128, 2048),
        master_weight,
        momentum,
        variance,
    )
    hbm = pl.BlockSpec(memory_space=pl.ANY)
    return pl.pallas_call(
        settle,
        out_shape=(
            jax.ShapeDtypeStruct((1024, 2048), BF16),
            jax.ShapeDtypeStruct((32, 2048), F32),
            jax.ShapeDtypeStruct((32, 2048), F32),
        ),
        in_specs=[hbm] * 3,
        out_specs=(hbm,) * 3,
        scratch_shapes=[
            pltpu.VMEM((1024, 2048), BF16),
            pltpu.VMEM((32, 2048), F32),
            pltpu.VMEM((32, 2048), F32),
            pltpu.SemaphoreType.DMA((6,)),
            pltpu.SemaphoreType.DMA((6,)),
        ],
        compiler_params=pltpu.CompilerParams(vmem_limit_bytes=60 * 2**20),
        cost_estimate=pl.CostEstimate(flops=0, bytes_accessed=9 * 10**6, transcendentals=0),
    )(new_w.reshape(1024, 2048), new_m, step)


def solution(mesh):
    return jax.shard_map(
        per_device,
        mesh=mesh,
        in_specs=(
            P(("dp", "rep"), None, None),
            P(("dp", "rep")),
            P(("dp", "rep"), None),
            P(("dp", "rep")),
            P(("dp", "rep")),
            P(("dp", "rep"), None),
            P("dp", None),
            P(),
            P("dp", None),
        ),
        out_specs=(P(), P("dp", None), P("dp", None)),
        check_vma=False,
    )
```

```python
import functools

import jax
import jax.numpy as jnp
from jax import lax
from jax.experimental import pallas as pl
from jax.experimental.pallas import tpu as pltpu
from jax.sharding import PartitionSpec as P

MESH = pl.DeviceIdType.MESH
F32 = jnp.float32
BF16 = jnp.bfloat16
momentum_decay = 0.9
learn_rate = 0.05
epsilon = 1e-06
normal_peak = 0.3989422804014327

GROUPS = (
    ((1, 1), (3, 3)),
    ((1, 2), (3, 0)),
    ((2, 1), (0, 3)),
    ((1, 3), (3, 1)),
    ((3, 2), (1, 0)),
    ((2, 3), (0, 1)),
    ((0, 2), (2, 0)),
    ((2, 2),),
)
MOVES = [(0, 0, 0), (0, 0, 1)]
for group in GROUPS:
    for core in (0, 1):
        for dy, dx in group:
            MOVES.append((dy, dx, core))

EDGES = (0, 18, 22, 26, 30, 32)
BUFFERS = len(EDGES) - 1
WINDOW = 8
AHEAD = 8
TILE = 1024


def gelu_slope(a):
    u = jnp.abs(a)
    d = 1.0 + u * (0.3275911 * 0.7071067811865476)
    t = pl.reciprocal(d, approx=True)
    t = t * (2.0 - d * t)
    e = jnp.exp2((a * a) * (-0.5 * 1.4426950408889634))
    poly = t * (
        0.5 * 0.254829592
        + t
        * (
            0.5 * -0.284496736
            + t * (0.5 * 1.421413741 + t * (0.5 * -1.453152027 + t * (0.5 * 1.061405429)))
        )
    )
    h = e * (poly - normal_peak * u)
    return jnp.where(a >= 0.0, 1.0 - h, h)


def kernel(
    counts,
    dest,
    dslot,
    segments,
    tok_hbm,
    cot_hbm,
    master,
    mom_hbm,
    variance,
    out_w,
    out_m,
    out_l,
    tok,
    stage,
    arr0,
    arr1,
    arr2,
    arr3,
    arr4,
    cot,
    w,
    gathered,
    acc,
    xs,
    xt,
    wt,
    metar,
    metas,
    orders,
    table,
    lengths,
    metasent,
    u,
    r1,
    s1,
    r2,
    s2,
    r3,
    r4,
    q,
    lsem,
    outsem,
    tss,
    tsr,
    mss,
    msr,
    gbs,
    gbr,
    gas,
    gar,
    gzs,
    gzr,
    gcs,
    gcr,
    c1s,
    c1r,
    c2s,
    c2r,
    c3s,
    c3r,
    c4s,
    c4r,
    qs,
    qr,
):
    me = lax.axis_index("dp")
    rep = lax.axis_index("rep")
    y = me // 8
    x = (me // 2) % 4
    c = me % 2
    a = (1 - c) * y + c * x
    b = (1 - c) * x + c * y
    sa = 4 * (1 - c) + c
    sb = 4 * c + (1 - c)
    arrs = (arr0, arr1, arr2, arr3, arr4)

    def place(ai, bi):
        return ai * sa + bi * sb

    def at_a(k):
        return (place((a + k) % 4, b) * 2 + c, rep)

    def at_b(k):
        return (place(a, (b + k) % 4) * 2 + c, rep)

    other = (y * 8 + x * 2 + 1 - c, rep)

    def copy(src, dst, ss, rs, dev):
        return pltpu.make_async_remote_copy(
            src_ref=src, dst_ref=dst, send_sem=ss, recv_sem=rs, device_id=dev, device_id_type=MESH
        )

    def peer(move):
        dy, dx, dc = move
        return (((y + dy) % 4) * 4 + (x + dx) % 4) * 2 + (c + dc) % 2

    def landing(j):
        n = max(i for i in range(BUFFERS) if EDGES[i] <= j)
        return arrs[n].at[j - EDGES[n]]

    ctok = pltpu.make_async_copy(tok_hbm, tok, lsem.at[0])
    ccot = pltpu.make_async_copy(cot_hbm, cot, lsem.at[1])
    cmom = pltpu.make_async_copy(mom_hbm, acc, lsem.at[2])
    ctok.start()

    w[y * 4 + x, c] = master[...].astype(BF16)
    barrier = pltpu.get_barrier_semaphore()

    @pl.loop(1, 32)
    def _(k):
        pl.semaphore_signal(barrier, inc=1, device_id=((me + k) % 32, rep), device_id_type=MESH)

    for k in range(1, 4):
        pl.semaphore_signal(barrier, inc=1, device_id=(me, (rep + k) % 4), device_id_type=MESH)

    @pl.loop(0, 32)
    def _(p):
        block, there, slot = jnp.int32(0), jnp.int32(0), jnp.int32(0)
        for i in range(16):
            same = jnp.where(dest[i] == p, 1, 0)
            block = block + same * i
            there = there + same
            slot = slot + same * (dslot[i] + 1)
        table[p] = jnp.minimum(block, 15)
        table[32 + p] = there
        table[64 + p] = slot

    pl.semaphore_wait(barrier, 34)

    quarter = pl.ds(pl.multiple_of(rep * 512, 512), 512)
    gb = []
    for k in range(1, 4):
        part = w.at[y * 4 + x, c, :, quarter]
        gb.append(copy(part, part, gbs.at[0, k - 1], gbr.at[0, k - 1], at_b(k)))
        gb[-1].start()

    ctok.wait()
    ccot.start()
    cmom.start()
    sends = [None]
    arr0[0] = tok[table[me]]
    metacopies = []
    ga = []
    gz = []
    gc = []

    def send(j):
        if j > WINDOW:
            sends[j - WINDOW].wait_send()
        p = peer(MOVES[j])
        spot = stage.at[(j - 1) % WINDOW]
        spot[...] = tok[table[p]]
        cp = copy(spot, landing(j), tss.at[j], tsr.at[j], (p, rep))
        cp.start()
        sends.append(cp)

    def prepare():
        for cp in metacopies:
            cp.wait()
        cmeta = pltpu.make_async_copy(metar, metas, lsem.at[3])
        cmeta.start()
        cmom.wait()

        @pl.loop(0, 32)
        def _(i):
            rows = pl.ds(pl.multiple_of(i * 32, 32), 32)
            acc[rows, :] = acc[rows, :] * (momentum_decay / (1.0 - momentum_decay))

        cmeta.wait()
        count = jnp.int32(0)
        for j in range(32):
            count = count + jnp.minimum(metas[j, 1, 0], 1)
            orders[16 + j] = count

        @pl.loop(0, 16)
        def _(k):
            found = jnp.int32(0)
            for j in range(32):
                found = found + jnp.where(orders[16 + j] <= k, 1, 0)
            orders[k] = found

        for cp in gz:
            cp.wait()
        part = w.at[:, c]
        gc.append(copy(part, part, gcs.at[0, 0], gcr.at[0, 0], other))
        gc[0].start()

    for j in range(1, EDGES[1] + AHEAD):
        send(j)
        if j == 4:
            for cp in gb:
                cp.wait()
            for k in range(1, 4):
                for bb in range(4):
                    part = w.at[place(a, bb), c, :, quarter]
                    ga.append(copy(part, part, gas.at[0, k - 1, bb], gar.at[0, k - 1, bb], at_a(k)))
                    ga[-1].start()
        if j == 6:
            for r in range(4):
                ids = segments[r : r + 1, :]
                live = lax.broadcasted_iota(jnp.int32, (1, 512), 1) < counts[r]
                found = jnp.zeros((1, 512), jnp.int32)
                for v in range(8):
                    hit = jnp.where((ids == v) & live, 1, 0)
                    found = found + hit * jnp.sum(hit, axis=1, keepdims=True)
                for i in range(4):
                    lengths[r * 4 + i] = jnp.broadcast_to(
                        found[:, i * 128 : (i + 1) * 128], (8, 128)
                    )
            line = lax.broadcasted_iota(jnp.int32, (8, 128), 0)
            for n in range(32):
                p = peer(MOVES[n])
                lens = lengths[table[p]] * table[32 + p]
                value = jnp.where(line == 0, lens, table[64 + p])
                if n == 0:
                    metar[0] = value
                else:
                    metasent[n] = value
                    metacopies.append(
                        copy(metasent.at[n], metar.at[n], mss.at[n], msr.at[n], (p, rep))
                    )
                    metacopies[-1].start()
        if j == 10:
            for cp in ga:
                cp.wait()
            for k in range(1, 4):
                part = w.at[:, c, :, quarter]
                gz.append(copy(part, part, gzs.at[k - 1], gzr.at[k - 1], (me, (rep + k) % 4)))
                gz[-1].start()
        if j == 17:
            prepare()
    ccot.wait()
    gc[0].wait()

    done = 0
    arrived = 1
    for number in range(BUFFERS):
        needed = EDGES[number + 1]
        while len(sends) < min(needed + AHEAD, 32):
            send(len(sends))
        while arrived < needed:
            sends[arrived].wait_recv()
            arrived += 1
        blocks = needed - 16 - done
        rowcount = blocks * 128
        slots = []
        for i in range(blocks):
            o = jnp.minimum(orders[done + i], 31)
            slots.append(jnp.clip(metas[o, 1, 0] - 1, 0, 15))
            block = arrs[0][jnp.minimum(o, EDGES[1] - 1)]
            for n in range(1, number + 1):
                at = jnp.clip(o - EDGES[n], 0, EDGES[n + 1] - EDGES[n] - 1)
                block = lax.select(o >= EDGES[n], arrs[n][at], block)
            xs[i * 128 : (i + 1) * 128, :] = block
            xt[:, i * 128 : (i + 1) * 128] = jnp.transpose(block)
            lens = metar[o][0:1, :]
            weight = jnp.where(lens > 0, 1.0 / jnp.maximum(lens, 1).astype(F32), 0.0)
            wt[i * 128 : (i + 1) * 128, :] = jnp.transpose(jnp.broadcast_to(weight, (128, 128)))
        done += blocks

        @pl.loop(0, 2048 // TILE)
        def _(n):
            cols = pl.ds(pl.multiple_of(n * TILE, TILE), TILE)
            pre = jnp.dot(
                xs[0:rowcount, :], w[:, :, :, cols].reshape(1024, TILE), preferred_element_type=F32
            )
            parts = []
            for i in range(blocks):
                rows = slice(i * 128, (i + 1) * 128)
                wide = jnp.concatenate([wt[rows, :]] * (TILE // 128), axis=1)
                ci = cot[slots[i], :, cols].astype(F32)
                parts.append((ci * gelu_slope(pre[rows]) * wide).astype(BF16))
            delta = jnp.concatenate(parts, axis=0)
            acc[:, cols] += jnp.dot(xt[:, 0:rowcount], delta, preferred_element_type=F32)

    for j in range(32 - WINDOW, 32):
        sends[j].wait_send()

    def squeezed(yx, core):
        rows = pl.ds(pl.multiple_of((yx * 2 + core) * 32, 32), 32)
        moment = acc[rows, :] * (1.0 - momentum_decay)
        scale = jnp.sum(jnp.abs(moment), axis=1, keepdims=True) * (1.0 / 2048)
        unit = jnp.tanh(moment * (1.0 / (scale + epsilon)))
        return scale.astype(BF16).astype(F32) * unit.astype(BF16).astype(F32)

    @pl.loop(0, 16)
    def _(i):
        yx = place((a + 1 + i // 4) % 4, i % 4)
        u[i] = squeezed(yx, 1 - c).astype(BF16)
        copy(u.at[i], r1.at[yx], c1s.at[i], c1r.at[yx], other).start()

    def add_core(k):
        @pl.loop(0, 4)
        def _(bb):
            yx = place((a + k) % 4, bb)
            copy(u.at[0], r1.at[yx], c1s.at[0], c1r.at[yx], other).wait_recv()
            s1[k, bb] = (squeezed(yx, c) + r1[yx].astype(F32)).astype(BF16)

    stage2 = []
    for k in (2, 1, 3, 0):
        add_core(k)
        if k:
            cp = copy(s1.at[k], r2.at[k - 1], c2s.at[k - 1], c2r.at[k - 1], at_a(k))
            cp.start()
            stage2.append(cp)
    for cp in stage2:
        cp.wait()

    def add_a(bi):
        total = s1[0, bi].astype(F32)
        for k in range(3):
            total = total + r2[k, bi].astype(F32)
        return total

    stage3 = []
    for k in (2, 1, 3):
        s2[k - 1] = add_a((b + k) % 4).astype(BF16)
        cp = copy(s2.at[k - 1], r3.at[k - 1], c3s.at[k - 1], c3r.at[k - 1], at_b(k))
        cp.start()
        stage3.append(cp)
    total = add_a(b)
    for cp in stage3:
        cp.wait()
    for k in range(3):
        total = total + r3[k].astype(F32)
    r4[rep] = total.astype(BF16)
    stage4 = []
    for k in (2, 1, 3):
        cp = copy(r4.at[rep], r4.at[rep], c4s.at[k - 1], c4r.at[k - 1], (me, (rep + k) % 4))
        cp.start()
        stage4.append(cp)
    for cp in stage4:
        cp.wait()
    average = (
        r4[0].astype(F32) + r4[1].astype(F32) + r4[2].astype(F32) + r4[3].astype(F32)
    ) * (1.0 / 128)
    scale = jnp.sum(jnp.abs(average), axis=1, keepdims=True) * (1.0 / 2048)
    moment = scale * jnp.tanh(average / (scale + epsilon))
    out_m[...] = moment
    direction = moment / (jnp.sqrt(variance[...]) + epsilon)
    gathered[y * 4 + x, c] = direction.astype(BF16)

    def group(ai, bi):
        return gathered.at[place(ai, bi), c]

    dcopies = []

    def to_a(bi):
        for k in (2, 1, 3):
            cp = copy(group(a, bi), group(a, bi), gas.at[1, k - 1, bi], gar.at[1, k - 1, bi], at_a(k))
            cp.start()
            dcopies.append(cp)

    def to_core(ai, bi):
        yx = place(ai, bi)
        copy(gathered.at[yx, c], gathered.at[yx, c], gcs.at[1, yx], gcr.at[1, yx], other).start()

    gb = {}
    for k in (2, 1, 3):
        gb[k] = copy(group(a, b), group(a, b), gbs.at[1, k - 1], gbr.at[1, k - 1], at_b(k))
        gb[k].start()
    to_a(b)

    def folded(v):
        line = jnp.sum(v, axis=0, keepdims=True)
        out = line[:, 0:128]
        for i in range(1, 16):
            out = out + line[:, i * 128 : (i + 1) * 128]
        return out

    q[me] = jnp.concatenate(
        [
            folded(master[...] * master[...]),
            folded(direction * direction),
            jnp.zeros((6, 128), F32),
        ],
        axis=0,
    )
    out_l[...] = direction
    scalars = []
    for j in range(1, 32):
        cp = copy(q.at[me], q.at[me], qs.at[j], qr.at[j], (peer(MOVES[j]), rep))
        cp.start()
        scalars.append(cp)

    to_core(a, b)
    for k in (1, 3, 2):
        gb[k].wait()
        to_a((b - k + 4) % 4)
        to_core(a, (b - k + 4) % 4)
    for cp in scalars:
        cp.wait()
    sums = jnp.sum(jnp.sum(q[...], axis=0), axis=1, keepdims=True)
    roots = jnp.sqrt(sums)
    ratio = roots[0:1, :] / (roots[1:2, :] + epsilon)
    out_l[...] = out_l[...] * ratio
    factor = learn_rate * ratio

    def update(yx, core):
        new = w[yx, core].astype(F32) - factor * gathered[yx, core].astype(F32)
        w[yx, core] = new.astype(BF16)
        at = yx * 2 + core
        pltpu.make_async_copy(w.at[yx, core], out_w.at[yx, core], outsem.at[at]).start()

    @pl.loop(0, 4)
    def _(i):
        update(place(a, i), c)

    def take(ai):
        @pl.loop(0, 4)
        def _(i):
            yx = ai * sb + ((a + i) % 4) * sa
            theirs = gathered.at[yx, 1 - c]
            copy(theirs, theirs, gcs.at[1, yx], gcr.at[1, yx], other).wait_recv()
            update(yx, 1 - c)

    pending = b
    for k in (1, 3, 2):
        ai = (a - k + 4) % 4

        @pl.loop(0, 4)
        def _(i):
            bi = (b + i) % 4
            copy(
                group(ai, bi), group(ai, bi), gas.at[1, k - 1, bi], gar.at[1, k - 1, bi], at_a(k)
            ).wait_recv()
            to_core(ai, bi)

        @pl.loop(0, 4)
        def _(i):
            update(place(ai, i), c)

        take(pending)
        pending = (b - k + 4) % 4
    take(pending)

    for cp in dcopies:
        cp.wait_send()

    @pl.loop(0, 16)
    def _(i):
        mine = gathered.at[i, c]
        copy(mine, mine, gcs.at[1, i], gcr.at[1, i], other).wait_send()
        copy(u.at[i], r1.at[i], c1s.at[i], c1r.at[i], other).wait_send()
        for core in range(2):
            pltpu.make_async_copy(
                w.at[i, core], out_w.at[i, core], outsem.at[i * 2 + core]
            ).wait()


def run(counts, dest, dslot, segments, tokens, cotangent, master, momentum, variance):
    sem = pltpu.SemaphoreType.DMA
    vmem = pl.BlockSpec(memory_space=pltpu.VMEM)
    smem = pl.BlockSpec(memory_space=pltpu.SMEM)
    hbm = pl.BlockSpec(memory_space=pl.ANY)
    return pl.pallas_call(
        kernel,
        out_shape=(
            jax.ShapeDtypeStruct((16, 2, 32, 2048), BF16),
            jax.ShapeDtypeStruct((32, 2048), F32),
            jax.ShapeDtypeStruct((32, 2048), F32),
        ),
        in_specs=[
            smem,
            smem,
            smem,
            vmem,
            hbm,
            hbm,
            vmem,
            hbm,
            vmem,
        ],
        out_specs=(hbm, vmem, vmem),
        scratch_shapes=[
            pltpu.VMEM((16, 128, 1024), BF16),
            pltpu.VMEM((WINDOW, 128, 1024), BF16),
            pltpu.VMEM((18, 128, 1024), BF16),
            pltpu.VMEM((4, 128, 1024), BF16),
            pltpu.VMEM((4, 128, 1024), BF16),
            pltpu.VMEM((4, 128, 1024), BF16),
            pltpu.VMEM((2, 128, 1024), BF16),
            pltpu.VMEM((16, 128, 2048), BF16),
            pltpu.VMEM((16, 2, 32, 2048), BF16),
            pltpu.VMEM((16, 2, 32, 2048), BF16),
            pltpu.VMEM((1024, 2048), F32),
            pltpu.VMEM((512, 1024), BF16),
            pltpu.VMEM((1024, 512), BF16),
            pltpu.VMEM((512, 128), F32),
            pltpu.VMEM((32, 8, 128), jnp.int32),
            pltpu.SMEM((32, 8, 128), jnp.int32),
            pltpu.SMEM((48,), jnp.int32),
            pltpu.SMEM((96,), jnp.int32),
            pltpu.VMEM((16, 8, 128), jnp.int32),
            pltpu.VMEM((32, 8, 128), jnp.int32),
            pltpu.VMEM((16, 32, 2048), BF16),
            pltpu.VMEM((16, 32, 2048), BF16),
            pltpu.VMEM((4, 4, 32, 2048), BF16),
            pltpu.VMEM((3, 4, 32, 2048), BF16),
            pltpu.VMEM((3, 32, 2048), BF16),
            pltpu.VMEM((3, 32, 2048), BF16),
            pltpu.VMEM((4, 32, 2048), BF16),
            pltpu.VMEM((32, 8, 128), F32),
            sem((4,)),
            sem((32,)),
            sem((32,)),
            sem((32,)),
            sem((32,)),
            sem((32,)),
            sem((2, 3)),
            sem((2, 3)),
            sem((2, 3, 4)),
            sem((2, 3, 4)),
            sem((3,)),
            sem((3,)),
            sem((2, 16)),
            sem((2, 16)),
            sem((16,)),
            sem((16,)),
            sem((3,)),
            sem((3,)),
            sem((3,)),
            sem((3,)),
            sem((3,)),
            sem((3,)),
            sem((32,)),
            sem((32,)),
        ],
        compiler_params=pltpu.CompilerParams(
            collective_id=1, has_side_effects=True, vmem_limit_bytes=63 * 2**20
        ),
        cost_estimate=pl.CostEstimate(
            flops=18 * 10**9, bytes_accessed=40 * 10**6, transcendentals=20 * 10**6
        ),
    )(counts, dest, dslot, segments, tokens, cotangent, master, momentum, variance)


def settle(w_in, m_in, l_in, w_out, m_out, l_out, w_mid, m_mid, l_mid, in_sem, out_sem):
    moves = []
    for i in range(4):
        rows = pl.ds(i * 256, 256)
        moves.append((w_in.at[rows], w_mid.at[rows], w_out.at[rows]))
    moves.append((m_in, m_mid, m_out))
    moves.append((l_in, l_mid, l_out))
    reads = [pltpu.make_async_copy(s, m, in_sem.at[i]) for i, (s, m, d) in enumerate(moves)]
    writes = [pltpu.make_async_copy(m, d, out_sem.at[i]) for i, (s, m, d) in enumerate(moves)]
    for cp in reads:
        cp.start()
    for read, write in zip(reads, writes):
        read.wait()
        write.start()
    for cp in writes:
        cp.wait()


def per_device(
    tokens,
    token_counts,
    segment_ids,
    dest_device,
    dest_slot,
    cotangent,
    master_weight,
    momentum,
    variance,
):
    new_w, new_m, step = run(
        token_counts,
        dest_device,
        dest_slot,
        segment_ids,
        tokens.reshape(16, 128, 1024),
        cotangent.reshape(16, 128, 2048),
        master_weight,
        momentum,
        variance,
    )
    hbm = pl.BlockSpec(memory_space=pl.ANY)
    return pl.pallas_call(
        settle,
        out_shape=(
            jax.ShapeDtypeStruct((1024, 2048), BF16),
            jax.ShapeDtypeStruct((32, 2048), F32),
            jax.ShapeDtypeStruct((32, 2048), F32),
        ),
        in_specs=[hbm] * 3,
        out_specs=(hbm,) * 3,
        scratch_shapes=[
            pltpu.VMEM((1024, 2048), BF16),
            pltpu.VMEM((32, 2048), F32),
            pltpu.VMEM((32, 2048), F32),
            pltpu.SemaphoreType.DMA((6,)),
            pltpu.SemaphoreType.DMA((6,)),
        ],
        compiler_params=pltpu.CompilerParams(vmem_limit_bytes=60 * 2**20),
        cost_estimate=pl.CostEstimate(flops=0, bytes_accessed=9 * 10**6, transcendentals=0),
    )(new_w.reshape(1024, 2048), new_m, step)


def solution(mesh):
    return jax.shard_map(
        per_device,
        mesh=mesh,
        in_specs=(
            P(("dp", "rep"), None, None),
            P(("dp", "rep")),
            P(("dp", "rep"), None),
            P(("dp", "rep")),
            P(("dp", "rep")),
            P(("dp", "rep"), None),
            P("dp", None),
            P(),
            P("dp", None),
        ),
        out_specs=(P(), P("dp", None), P("dp", None)),
        check_vma=False,
    )
```
